512 devices in a mesh: chan: 32 (over z_lo, x), win: 16 (over z_hi, y, core).
Axes of the slice: x: 4, y: 4, z: 16 (z_hi: 2, z_lo: 8; z = z_hi * 8 + z_lo), core: 2. Of those that a mesh axis runs over, the one named last changes fastest.
Arguments:
- records: bfloat16 [96, 256, 32, 1024], P('chan', None, 'win'), may hold values from -20 to 20
- pairs: int32 [80, 2], replicated, may hold values from 0 to 95, as said below
- owner: int32 [80], replicated, may hold values from 0 to 31, as said below
Outputs:
- cross_spectra: float32 [128, 256, 1024], P('chan', 'win')
The draws below stay inside these ranges and needn't reach their ends.
Inputs may be any that keep to these rules, and one draw needn't show every extreme that they name: `pairs`: each row holds two channel blocks a < b with b - a from 1 to 3. owner[p] is the chan index of a device holding some block from pairs[p, 0] to pairs[p, 1]; every owner has 2 to 4 pairs.
All inputs are finite; a program needn't handle non-finite values.
Results may differ from the reference program's by a relative error of at most 0.0055.
Values may be sent and summed in bfloat16 or wider, within the bound.
No kernel may reach another device: no remote copies, remote signals or barrier semaphores. Data moves between devices by JAX's collectives and lax.ppermute only.
A program may use at most 64 MiB of HBM per device.

```python
import math
import jax
import jax.numpy as jnp
from jax import lax

CH = 256
L = 1024
F = 512
BLK_DEV = 3
REACH = 3
PCAP = 4
BLOCKS = 96
WINDOWS = 32
PAIRS = 80
N_CHAN = 32


def pair_table(key):
    owners = BLOCKS // BLK_DEV
    keys = jax.random.split(key, 5)
    pattern = jnp.tile(jnp.array([2, 2, 2, 4], dtype=jnp.int32), owners // 4)
    counts = pattern[jax.random.permutation(keys[0], owners)]
    device_ids = jnp.arange(owners, dtype=jnp.int32)[:, None] * jnp.ones((1, PCAP), dtype=jnp.int32)
    slot_ids = jnp.arange(PCAP, dtype=jnp.int32)[None, :] * jnp.ones((owners, 1), dtype=jnp.int32)
    inner = device_ids * BLK_DEV + jax.random.randint(keys[1], (owners, PCAP), 0, BLK_DEV)
    anchor = jnp.where(slot_ids == 0, device_ids * BLK_DEV, jnp.where(slot_ids == 1, device_ids * BLK_DEV + BLK_DEV - 1, inner))
    spread = jnp.where(slot_ids < 2, REACH, jax.random.randint(keys[2], (owners, PCAP), 1, REACH + 1))
    backward = jax.random.randint(keys[3], (owners, PCAP), 0, spread + 1)
    backward = jnp.where(slot_ids == 0, jnp.maximum(backward, 1), jnp.where(slot_ids == 1, jnp.minimum(backward, REACH - 1), backward))
    lower = jnp.clip(anchor - backward, 0, BLOCKS - 1 - spread)
    upper = lower + spread
    used = slot_ids < counts[:, None]
    scores = jnp.where(used, 0, owners * PCAP) + jax.random.permutation(keys[4], owners * PCAP).reshape(owners, PCAP)
    ordering = jnp.argsort(scores.reshape(-1))[:PAIRS]
    pair_rows = jnp.stack([lower.reshape(-1)[ordering], upper.reshape(-1)[ordering]], axis=1).astype(jnp.int32)
    owner_rows = device_ids.reshape(-1)[ordering].astype(jnp.int32)
    return (pair_rows, owner_rows)


def draw_pairs(key, part):
    pair_rows, owner_rows = pair_table(key)
    return pair_rows


def draw_owner(key, part):
    pair_rows, owner_rows = pair_table(key)
    return owner_rows


def draw_records(key, part):
    key = jax.random.fold_in(key, 5)
    keys = jax.random.split(key, 3)
    full_shape = (BLOCKS, CH, WINDOWS, L)
    channel_gain = jnp.exp(jax.random.uniform(keys[0], (BLOCKS, CH, 1, 1), minval=math.log(0.2), maxval=math.log(3.0)))
    window_gain = jnp.exp(jax.random.uniform(keys[1], (1, 1, WINDOWS, 1), minval=math.log(0.5), maxval=math.log(2.0)))
    values = jax.random.normal(keys[2], full_shape) * channel_gain * window_gain
    return jnp.clip(values, -20.0, 20.0).astype(jnp.bfloat16)


def setup_inputs(seed: int = 0) -> dict:
    arg_keys = jax.random.split(jax.random.key(seed), 4)
    return {
        "records": draw_records(jax.random.fold_in(arg_keys[3], 71), 0),
        "pairs": draw_pairs(jax.random.fold_in(arg_keys[3], 71), 0),
        "owner": draw_owner(jax.random.fold_in(arg_keys[3], 71), 0),
    }


def basis_table(length, bin_count):
    sample_ids = jnp.arange(length, dtype=jnp.int32)
    bin_ids = jnp.arange(bin_count, dtype=jnp.int32)
    phases = (sample_ids[:, None] * bin_ids[None, :] % length).astype(jnp.float32) * (2.0 * math.pi / length)
    hann_taper = 0.5 - 0.5 * jnp.cos(sample_ids.astype(jnp.float32) * (2.0 * math.pi / length))
    return jnp.concatenate([hann_taper[:, None] * jnp.cos(phases), -hann_taper[:, None] * jnp.sin(phases)], axis=1).astype(jnp.bfloat16)

def whitened_rows(row_data, basis):
    spectrum = jnp.dot(row_data, basis, preferred_element_type=jnp.float32)
    power_mean = lax.optimization_barrier(jnp.mean(spectrum * spectrum, axis=-1, keepdims=True))
    return (spectrum * lax.rsqrt(power_mean + 1e-06)).astype(jnp.bfloat16)

def cross_sum(first_spec, second_spec, bin_count):
    first_spec = first_spec.astype(jnp.float32)
    second_spec = second_spec.astype(jnp.float32)
    first_real = first_spec[..., :bin_count]
    first_imag = first_spec[..., bin_count:]
    second_real = second_spec[..., :bin_count]
    second_imag = second_spec[..., bin_count:]
    real_part = lax.optimization_barrier(jnp.sum(first_real * second_real + first_imag * second_imag, axis=-2))
    imag_part = lax.optimization_barrier(jnp.sum(first_imag * second_real - first_real * second_imag, axis=-2))
    return jnp.concatenate([real_part, imag_part], axis=-1)

def reference(records, pairs, owner):
    basis = basis_table(L, F)

    def one_block(block_rows):
        flat_rows = block_rows.reshape(CH * WINDOWS, L)
        return whitened_rows(flat_rows, basis).reshape(CH, WINDOWS, 2 * F)
    spectra = lax.map(one_block, records)
    owner_hot = (owner[:, None] == jnp.arange(N_CHAN, dtype=jnp.int32)[None, :]).astype(jnp.int32)
    earlier = jnp.cumsum(owner_hot, axis=0) - owner_hot
    ranking = lax.optimization_barrier(jnp.sum(earlier * owner_hot, axis=1)).astype(jnp.int32)
    slot_of = (owner * PCAP + ranking).astype(jnp.int32)
    slot_pair = jnp.full((N_CHAN * PCAP,), -1, dtype=jnp.int32).at[slot_of].set(jnp.arange(PAIRS, dtype=jnp.int32))

    def one_slot(pair_index):
        safe_index = jnp.maximum(pair_index, 0)
        first_spec = spectra[pairs[safe_index, 0]]
        second_spec = spectra[pairs[safe_index, 1]]
        result = cross_sum(first_spec, second_spec, F)
        return jnp.where(pair_index >= 0, result, jnp.zeros_like(result))
    return lax.map(one_slot, slot_pair)
```

```python
import math

import jax
import jax.numpy as jnp
import ml_dtypes
import numpy as np
from jax import lax
from jax.experimental import pallas as pl
from jax.experimental.pallas import tpu as pltpu
from jax.sharding import PartitionSpec as P

PCAP = 4
BLOCKS = 3
CHAN = 32
CHUNKS = 2
LENGTH = 1024
BINS = 512
ROWS = 256 // CHUNKS
VMEM = pl.BlockSpec(memory_space=pltpu.VMEM)
SMEM = pl.BlockSpec(memory_space=pltpu.SMEM)
ANY = pl.BlockSpec(memory_space=pl.ANY)
PARAMS = pltpu.CompilerParams(vmem_limit_bytes=40 << 20)


def basis_table():
    sample_ids = np.arange(LENGTH, dtype=np.int32)
    bin_ids = np.arange(BINS, dtype=np.int32)
    step = np.float32(2.0 * math.pi / LENGTH)
    phases = (sample_ids[:, None] * bin_ids[None, :] % LENGTH).astype(np.float32) * step
    taper = np.float32(0.5) - np.float32(0.5) * np.cos(sample_ids.astype(np.float32) * step)
    table = np.concatenate([taper[:, None] * np.cos(phases), -taper[:, None] * np.sin(phases)], axis=1)
    return table.astype(ml_dtypes.bfloat16)


def lanes(pairs, owner):
    first, second = pairs[:, 0], pairs[:, 1]
    ids = jnp.arange(BLOCKS * CHAN, dtype=jnp.int32)
    right = jnp.any((first[None, :] == ids[:, None]) & (owner[None, :] == ids[:, None] // BLOCKS + 1), axis=1)
    left = jnp.any((second[None, :] == ids[:, None]) & (owner[None, :] == ids[:, None] // BLOCKS - 1), axis=1)
    right = right.astype(jnp.int32).reshape(CHAN, BLOCKS)
    left = left.astype(jnp.int32).reshape(CHAN, BLOCKS)
    most = jnp.maximum(jnp.max(jnp.sum(right, axis=1)), jnp.max(jnp.sum(left, axis=1)))
    return right, left, most


def tables(pairs, owner, right, left, width):
    me = lax.axis_index("chan")
    if width < BLOCKS:
        place_right = jnp.cumsum(right, axis=1) - right
        place_left = jnp.cumsum(left, axis=1) - left
    else:
        place_right = place_left = jnp.broadcast_to(jnp.arange(BLOCKS, dtype=jnp.int32), (CHAN, BLOCKS))
        right = left = jnp.ones((CHAN, BLOCKS), jnp.int32)
    spots = jnp.arange(width, dtype=jnp.int32)
    block_ids = jnp.arange(BLOCKS, dtype=jnp.int32)

    def row(table, at):
        return jnp.sum(jnp.where(jnp.arange(CHAN)[:, None] == at, table, 0), axis=0)

    def chosen(need, place):
        hit = (row(need, me)[None, :] > 0) & (row(place, me)[None, :] == spots[:, None])
        return jnp.sum(jnp.where(hit, block_ids[None, :], 0), axis=1)

    send = jnp.concatenate([chosen(right, place_right), chosen(left, place_left)])
    mine = (owner == me).astype(jnp.int32)
    ranking = jnp.cumsum(mine) - mine
    slots = jnp.arange(PCAP, dtype=jnp.int32)
    picked = mine[None, :] * (ranking[None, :] == slots[:, None]).astype(jnp.int32)
    used = jnp.sum(picked, axis=1)
    first = jnp.sum(picked * pairs[:, 0][None, :], axis=1) - me * BLOCKS
    second = jnp.sum(picked * pairs[:, 1][None, :], axis=1) - me * BLOCKS

    def look(table, index):
        return jnp.sum(jnp.where(index[:, None] == block_ids[None, :], table[None, :], 0), axis=1)

    from_left = BLOCKS + look(row(place_right, me - 1), first + BLOCKS)
    from_right = BLOCKS + width + look(row(place_left, me + 1), second - BLOCKS)
    a = jnp.where(first < 0, from_left, first)
    b = jnp.where(second >= BLOCKS, from_right, second)
    a = jnp.where(used > 0, jnp.clip(a, 0, BLOCKS + 2 * width - 1), 0)
    b = jnp.where(used > 0, jnp.clip(b, 0, BLOCKS + 2 * width - 1), 0)
    return send.astype(jnp.int32), jnp.concatenate([a, b, used]).astype(jnp.int32)


def spectra_kernel(chunk, width, info, x, basis, own0, own1, right0, right1, left0, left1, xbuf, bbuf, spec, xsem, bsem, osem, lsem):
    core = info[2 * width]

    def load(side, block):
        at = (core + side) % 2
        return pltpu.make_async_copy(x.at[block, :, at, chunk], xbuf.at[side, block], xsem.at[side, block])

    table = pltpu.make_async_copy(basis, bbuf, bsem)
    load(0, 0).start()
    table.start()
    for side in range(2):
        for block in range(BLOCKS):
            if (side, block) != (0, 0):
                load(side, block).start()
    table.wait()
    owns = (own0, own1)
    lane_refs = ((right0, right1), (left0, left1))
    for side in range(2):
        for block in range(BLOCKS):
            load(side, block).wait()
            rows = xbuf[side, block].reshape(ROWS, LENGTH)
            spectrum = jnp.dot(rows, bbuf[...], preferred_element_type=jnp.float32)
            power_mean = jnp.mean(spectrum * spectrum, axis=-1, keepdims=True)
            spec[side, block] = (spectrum * lax.rsqrt(power_mean + 1e-06)).astype(jnp.bfloat16)
            pltpu.make_async_copy(spec.at[side, block], owns[side].at[block], osem.at[side, block]).start()
            for way in range(2):
                for spot in range(width):

                    @pl.when(info[way * width + spot] == block)
                    def _(side=side, block=block, way=way, spot=spot):
                        pltpu.make_async_copy(
                            spec.at[side, block], lane_refs[way][side].at[spot], lsem.at[side, way, spot]
                        ).start()

    for side in range(2):
        for block in range(BLOCKS):
            pltpu.make_async_copy(spec.at[side, block], owns[side].at[block], osem.at[side, block]).wait()
        for way in range(2):
            for spot in range(width):
                pltpu.make_async_copy(
                    spec.at[side, 0], lane_refs[way][side].at[spot], lsem.at[side, way, spot]
                ).wait()


def spectra(chunk, width, info, x, basis):
    own = jax.ShapeDtypeStruct((BLOCKS, ROWS, LENGTH), jnp.bfloat16)
    lane = jax.ShapeDtypeStruct((width, ROWS, LENGTH), jnp.bfloat16)
    return pl.pallas_call(
        lambda *refs: spectra_kernel(chunk, width, *refs),
        out_shape=(own, own, lane, lane, lane, lane),
        in_specs=[SMEM, ANY, ANY],
        out_specs=[ANY] * 6,
        scratch_shapes=[
            pltpu.VMEM((2, BLOCKS, 8, 16 // CHUNKS, 2, LENGTH), jnp.bfloat16),
            pltpu.VMEM((LENGTH, LENGTH), jnp.bfloat16),
            pltpu.VMEM((2, BLOCKS, ROWS, LENGTH), jnp.bfloat16),
            pltpu.SemaphoreType.DMA((2, BLOCKS)),
            pltpu.SemaphoreType.DMA,
            pltpu.SemaphoreType.DMA((2, BLOCKS)),
            pltpu.SemaphoreType.DMA((2, 2, width)),
        ],
        compiler_params=PARAMS,
        cost_estimate=pl.CostEstimate(flops=2 * 6 * ROWS * LENGTH * LENGTH, bytes_accessed=8 << 20, transcendentals=0),
        name="spectra",
    )(info, x, basis)


def products_kernel(width, info, own0, own1, l0, l1, r0, r1, out, buf, acc, sems):
    copies = []
    for side, (own, low, high) in enumerate(((own0, l0, r0), (own1, l1, r1))):
        for part, (ref, start, count) in enumerate(
            ((own, 0, BLOCKS), (low, BLOCKS, width), (high, BLOCKS + width, width))
        ):
            copies.append(pltpu.make_async_copy(ref, buf.at[side, pl.ds(start, count)], sems.at[side, part]))
    for copy in copies:
        copy.start()
    for copy in copies:
        copy.wait()
    half = 16 // CHUNKS

    @pl.loop(0, PCAP)
    def _(slot):
        a, b, used = info[slot], info[PCAP + slot], info[2 * PCAP + slot]

        @pl.when(used > 0)
        def _():
            @pl.loop(0, 4)
            def _(y):
                for lane in range(BINS // 128):
                    re_lanes = pl.ds(lane * 128, 128)
                    im_lanes = pl.ds(BINS + lane * 128, 128)
                    for z in range(2):
                        at = pl.ds(pl.multiple_of((z * 4 + y) * 2 * half, 2 * half), 2 * half)
                        real = imag = None
                        for side in range(2):
                            a_re = buf[side, a, at, re_lanes].astype(jnp.float32)
                            a_im = buf[side, a, at, im_lanes].astype(jnp.float32)
                            b_re = buf[side, b, at, re_lanes].astype(jnp.float32)
                            b_im = buf[side, b, at, im_lanes].astype(jnp.float32)
                            re = a_re * b_re + a_im * b_im
                            im = a_im * b_re - a_re * b_im
                            real = re if real is None else real + re
                            imag = im if imag is None else imag + im
                        acc[lane, z, 0] = real
                        acc[lane, z, 1] = imag
                    for part, lanes_at in ((0, re_lanes), (1, im_lanes)):
                        sums = [
                            acc[lane, z, part, pl.ds(0, half, 2), :] + acc[lane, z, part, pl.ds(1, half, 2), :]
                            for z in range(2)
                        ]
                        out[y, slot, :, lanes_at] = jnp.concatenate(sums, axis=0).astype(jnp.bfloat16)

        @pl.when(used == 0)
        def _():
            @pl.loop(0, 4)
            def _(y):
                out[y, slot] = jnp.zeros((2 * half, LENGTH), jnp.bfloat16)


def products(width, info, *arrays):
    half = 16 // CHUNKS
    return pl.pallas_call(
        lambda *refs: products_kernel(width, *refs),
        out_shape=jax.ShapeDtypeStruct((4, PCAP, 2 * half, LENGTH), jnp.bfloat16),
        in_specs=[SMEM] + [ANY] * 6,
        out_specs=VMEM,
        scratch_shapes=[
            pltpu.VMEM((2, BLOCKS + 2 * width, ROWS, LENGTH), jnp.bfloat16),
            pltpu.VMEM((BINS // 128, 2, 2, 2 * half, 128), jnp.float32),
            pltpu.SemaphoreType.DMA((2, 3)),
        ],
        compiler_params=PARAMS,
        cost_estimate=pl.CostEstimate(flops=1 << 25, bytes_accessed=8 << 20, transcendentals=0),
        name="products",
    )(info, *arrays)


def routes():
    def both(step, flip):
        out = []
        for chan in range(CHAN):
            if 0 <= chan + step < CHAN:
                out += [(chan * 16 + win, (chan + step) * 16 + (win ^ flip)) for win in range(16)]
        return out

    return both


def path(records, pairs, owner, right, left, width):
    route = routes()
    axes = ("chan", "win")
    win = lax.axis_index("win")
    core = win % 2
    far = win // 8
    send, slots = tables(pairs, owner, right, left, width)
    send = jnp.concatenate([send, core[None].astype(jnp.int32)])
    basis = jnp.asarray(basis_table())
    x = records.reshape(BLOCKS, 8, 2, CHUNKS, 16 // CHUNKS, 2, LENGTH)
    half = 16 // CHUNKS
    ready = []
    for chunk in range(CHUNKS):
        own0, own1, r0, r1, l0, l1 = spectra(chunk, width, send, x, basis)
        low0 = lax.ppermute(r0, axes, route(1, 0))
        low1 = lax.ppermute(r1, axes, route(1, 1))
        high0 = lax.ppermute(l0, axes, route(-1, 0))
        high1 = lax.ppermute(l1, axes, route(-1, 1))
        other = lax.ppermute(own1, axes, route(0, 1))
        ready.append((own0, other, low0, low1, high0, high1))
    y_groups = [[z * 8 + y * 2 + c for y in range(4)] for z in range(2) for c in range(2)]
    z_groups = [[z * 8 + y * 2 + c for z in range(2)] for y in range(4) for c in range(2)]
    keep, give = [], []
    for chunk in range(CHUNKS):
        part = products(width, slots, *ready[chunk])
        part = lax.all_to_all(part, "win", 0, 0, tiled=True, axis_index_groups=y_groups)
        total = jnp.sum(part.astype(jnp.float32), axis=0).reshape(PCAP, 2, half, LENGTH)
        keep.append(lax.dynamic_index_in_dim(total, far, axis=1, keepdims=False))
        give.append(lax.dynamic_index_in_dim(total, 1 - far, axis=1, keepdims=False).astype(jnp.bfloat16))
    keep = jnp.concatenate(keep, axis=1)
    give = jnp.concatenate(give, axis=1)
    got = lax.all_gather(give, "win", axis=0, tiled=False, axis_index_groups=z_groups)
    got = lax.dynamic_index_in_dim(got, 1 - far, axis=0, keepdims=False)
    return keep + got.astype(jnp.float32)


def local(records, pairs, owner):
    right, left, most = lanes(pairs, owner)
    return lax.cond(
        most <= 2,
        lambda: path(records, pairs, owner, right, left, 2),
        lambda: path(records, pairs, owner, right, left, 3),
    )


def solution(mesh):
    return jax.shard_map(
        local,
        mesh=mesh,
        in_specs=(P("chan", None, "win", None), P(), P()),
        out_specs=P("chan", "win", None),
        check_vma=False,
    )
```

```python
import math

import jax
import jax.numpy as jnp
import ml_dtypes
import numpy as np
from jax import lax
from jax.experimental import pallas as pl
from jax.experimental.pallas import tpu as pltpu
from jax.sharding import PartitionSpec as P

PCAP = 4
BLOCKS = 3
CHAN = 32
CHUNKS = 2
LENGTH = 1024
BINS = 512
HALF = 16 // CHUNKS
ROWS = 512 // CHUNKS
SIDE = ROWS // 2
VMEM = pl.BlockSpec(memory_space=pltpu.VMEM)
SMEM = pl.BlockSpec(memory_space=pltpu.SMEM)
ANY = pl.BlockSpec(memory_space=pl.ANY)
PARAMS = pltpu.CompilerParams(vmem_limit_bytes=40 << 20)


def basis_table():
    sample_ids = np.arange(LENGTH, dtype=np.int32)
    bin_ids = np.arange(BINS, dtype=np.int32)
    step = np.float32(2.0 * math.pi / LENGTH)
    phases = (sample_ids[:, None] * bin_ids[None, :] % LENGTH).astype(np.float32) * step
    taper = np.float32(0.5) - np.float32(0.5) * np.cos(sample_ids.astype(np.float32) * step)
    table = np.concatenate([taper[:, None] * np.cos(phases), -taper[:, None] * np.sin(phases)], axis=1)
    return table.astype(ml_dtypes.bfloat16)


def most_needed(pairs, owner):
    first, second = pairs[:, 0], pairs[:, 1]
    ids = jnp.arange(BLOCKS * CHAN, dtype=jnp.int32)
    right = (first[None, :] == ids[:, None]) & (owner[None, :] == ids[:, None] // BLOCKS + 1)
    left = (second[None, :] == ids[:, None]) & (owner[None, :] == ids[:, None] // BLOCKS - 1)
    need = jnp.stack([jnp.any(right, axis=1), jnp.any(left, axis=1)]).astype(jnp.int32)
    return jnp.max(jnp.sum(need.reshape(2, CHAN, BLOCKS), axis=2))


RIGHT, LEFT, FIRST, SECOND, USED, TABLE = 0, 3, 6, 10, 14, 18


def fill_table(width, where, pairs, owner, info, seen):
    me = where[0]

    def bit(block):
        return jnp.where(block == 0, 1, jnp.where(block == 1, 2, jnp.where(block == 2, 4, 0)))

    def step(p, carry):
        to_right, to_left, of_left, of_right, count = carry
        first = pairs[0, p] - me * BLOCKS
        second = pairs[1, p] - me * BLOCKS
        apart = owner[p] - me
        to_right |= jnp.where(apart == 1, bit(first), 0)
        to_left |= jnp.where(apart == -1, bit(second), 0)
        mine = apart == 0
        of_left |= jnp.where(mine, bit(first + BLOCKS), 0)
        of_right |= jnp.where(mine, bit(second - BLOCKS), 0)

        @pl.when(mine & (count < PCAP))
        def _():
            seen[0, count] = first
            seen[1, count] = second

        return to_right, to_left, of_left, of_right, count + mine.astype(jnp.int32)

    zero = jnp.int32(0)
    for slot in range(PCAP):
        seen[0, slot] = zero
        seen[1, slot] = zero
    to_right, to_left, of_left, of_right, count = lax.fori_loop(
        0, owner.shape[0], step, (zero, zero, zero, zero, zero), unroll=4
    )

    def spot(mask, block):
        if width == BLOCKS:
            return block
        low = mask & 1
        return jnp.where(block == 0, 0, jnp.where(block == 1, low, jnp.minimum(low + ((mask >> 1) & 1), width - 1)))

    for base, mask in ((RIGHT, to_right), (LEFT, to_left)):
        if width == BLOCKS:
            picks = (0, 1, 2)
        else:
            lowest = jnp.where((mask & 1) > 0, 0, jnp.where((mask & 2) > 0, 1, jnp.where((mask & 4) > 0, 2, 0)))
            next_one = jnp.where((mask & 3) == 3, 1, jnp.where((mask == 5) | (mask == 6), 2, 0))
            picks = (lowest, next_one, 0)
        for i in range(3):
            info[base + i] = jnp.int32(picks[i])
    for slot in range(PCAP):
        used = count > slot
        first = jnp.where(used, seen[0, slot], 0)
        second = jnp.where(used, seen[1, slot], 0)
        info[FIRST + slot] = jnp.where(first < 0, BLOCKS + spot(of_left, first + BLOCKS), first)
        info[SECOND + slot] = jnp.where(
            second >= BLOCKS, BLOCKS + width + spot(of_right, second - BLOCKS), second
        )
        info[USED + slot] = used.astype(jnp.int32)


def load_and_whiten(load, basis, xbuf, bbuf, bsem, spec, meanwhile, done):
    table = pltpu.make_async_copy(basis, bbuf, bsem)
    for copy in load(0):
        copy.start()
    table.start()
    for block in range(1, BLOCKS):
        for copy in load(block):
            copy.start()
    meanwhile()
    for block in range(BLOCKS):
        for copy in load(block):
            copy.wait()
        if block == 0:
            table.wait()
        rows = xbuf[block].reshape(ROWS, LENGTH)
        spectrum = jnp.dot(rows, bbuf[...], preferred_element_type=jnp.float32)
        power_mean = jnp.mean(spectrum * spectrum, axis=-1, keepdims=True)
        spec[block] = (spectrum * lax.rsqrt(power_mean + 1e-06)).astype(jnp.bfloat16)
        done(block)


def spectra_kernel(chunk, width, where, pairs, owner, x, basis, own, right, left, info, xbuf, bbuf, spec, xsem, bsem, osem, lsem, seen):
    def load(block):
        return [pltpu.make_async_copy(x.at[block, :, chunk], xbuf.at[block], xsem.at[block])]

    def lane_copy(way, spot, block):
        return pltpu.make_async_copy(spec.at[block], (right, left)[way].at[spot], lsem.at[way, spot])

    def own_copy(block):
        return pltpu.make_async_copy(spec.at[block], own.at[block], osem.at[block])

    load_and_whiten(
        load, basis, xbuf, bbuf, bsem, spec,
        lambda: fill_table(width, where, pairs, owner, info, seen),
        lambda block: own_copy(block).start(),
    )
    for way in range(2):
        for spot in range(width):
            lane_copy(way, spot, info[way * 3 + spot]).start()
    for block in range(BLOCKS):
        own_copy(block).wait()
    for way in range(2):
        for spot in range(width):
            lane_copy(way, spot, 0).wait()


COST = pl.CostEstimate(flops=2 * 3 * ROWS * LENGTH * LENGTH, bytes_accessed=8 << 20, transcendentals=0)


def spectra(chunk, width, where, pairs, owner, x, basis):
    own = jax.ShapeDtypeStruct((BLOCKS, ROWS, LENGTH), jnp.bfloat16)
    lane = jax.ShapeDtypeStruct((width, ROWS, LENGTH), jnp.bfloat16)
    return pl.pallas_call(
        lambda *refs: spectra_kernel(chunk, width, *refs),
        out_shape=(own, lane, lane, jax.ShapeDtypeStruct((TABLE,), jnp.int32)),
        in_specs=[SMEM] * 3 + [ANY, ANY],
        out_specs=[ANY] * 3 + [SMEM],
        scratch_shapes=[
            pltpu.VMEM((BLOCKS, 16, HALF, 2, LENGTH), jnp.bfloat16),
            pltpu.VMEM((LENGTH, LENGTH), jnp.bfloat16),
            pltpu.VMEM((BLOCKS, ROWS, LENGTH), jnp.bfloat16),
            pltpu.SemaphoreType.DMA((BLOCKS,)),
            pltpu.SemaphoreType.DMA,
            pltpu.SemaphoreType.DMA((BLOCKS,)),
            pltpu.SemaphoreType.DMA((2, width)),
            pltpu.SMEM((2, PCAP), jnp.int32),
        ],
        compiler_params=PARAMS,
        cost_estimate=COST,
        name="spectra",
    )(where, pairs, owner, x, basis)


def split_kernel(chunk, where, x, basis, same, other, xbuf, bbuf, spec, xsem, bsem, osem):
    core = where[1]

    def load(block):
        return [
            pltpu.make_async_copy(x.at[block, :, (core + side) % 2, chunk], xbuf.at[block, side], xsem.at[block, side])
            for side in range(2)
        ]

    def own_copies(block):
        return [
            pltpu.make_async_copy(spec.at[block, pl.ds(side * SIDE, SIDE)], ref.at[block], osem.at[block, side])
            for side, ref in enumerate((same, other))
        ]

    def done(block):
        for copy in own_copies(block):
            copy.start()

    load_and_whiten(load, basis, xbuf, bbuf, bsem, spec, lambda: None, done)
    for block in range(BLOCKS):
        for copy in own_copies(block):
            copy.wait()


def split_spectra(chunk, where, x, basis):
    own = jax.ShapeDtypeStruct((BLOCKS, SIDE, LENGTH), jnp.bfloat16)
    return pl.pallas_call(
        lambda *refs: split_kernel(chunk, *refs),
        out_shape=(own, own),
        in_specs=[SMEM] + [ANY, ANY],
        out_specs=[ANY] * 2,
        scratch_shapes=[
            pltpu.VMEM((BLOCKS, 2, 8, HALF, 2, LENGTH), jnp.bfloat16),
            pltpu.VMEM((LENGTH, LENGTH), jnp.bfloat16),
            pltpu.VMEM((BLOCKS, ROWS, LENGTH), jnp.bfloat16),
            pltpu.SemaphoreType.DMA((BLOCKS, 2)),
            pltpu.SemaphoreType.DMA,
            pltpu.SemaphoreType.DMA((BLOCKS, 2)),
        ],
        compiler_params=PARAMS,
        cost_estimate=COST,
        name="split_spectra",
    )(where, x, basis)


def lanes_kernel(width, info, same, other, right, left, sems):
    def copies(block_of):
        return [
            pltpu.make_async_copy(ref.at[block_of(way, spot)], lane.at[side, spot], sems.at[way, spot, side])
            for way, lane in enumerate((right, left))
            for spot in range(width)
            for side, ref in enumerate((same, other))
        ]

    for copy in copies(lambda way, spot: info[way * 3 + spot]):
        copy.start()
    for copy in copies(lambda way, spot: 0):
        copy.wait()


def lanes(width, info, same, other):
    lane = jax.ShapeDtypeStruct((2, width, SIDE, LENGTH), jnp.bfloat16)
    return pl.pallas_call(
        lambda *refs: lanes_kernel(width, *refs),
        out_shape=(lane, lane),
        in_specs=[SMEM] + [ANY, ANY],
        out_specs=[ANY] * 2,
        scratch_shapes=[pltpu.SemaphoreType.DMA((2, width, 2))],
        compiler_params=PARAMS,
        cost_estimate=pl.CostEstimate(flops=0, bytes_accessed=4 << 20, transcendentals=0),
        name="lanes",
    )(info, same, other)


def products_kernel(width, sides, *refs):
    info, owns, (low, high, out, buf, acc, sems) = refs[0], refs[1 : 1 + sides], refs[1 + sides :]
    peers = 8 // sides
    copies = []
    for side in range(sides):
        parts = (
            (owns[side], 0, BLOCKS),
            (low.at[side], BLOCKS, width),
            (high.at[side], BLOCKS + width, width),
        )
        for part, (ref, start, count) in enumerate(parts):
            copies.append(pltpu.make_async_copy(ref, buf.at[side, pl.ds(start, count)], sems.at[side, part]))
    for copy in copies:
        copy.start()
    for copy in copies:
        copy.wait()

    @pl.loop(0, PCAP)
    def _(slot):
        a, b, used = info[FIRST + slot], info[SECOND + slot], info[USED + slot]

        @pl.when(used > 0)
        def _():
            @pl.loop(0, peers)
            def _(peer):
                for lane in range(BINS // 128):
                    re_lanes = pl.ds(lane * 128, 128)
                    im_lanes = pl.ds(BINS + lane * 128, 128)
                    for z in range(2):
                        at = pl.ds(pl.multiple_of((z * peers + peer) * 2 * HALF, 2 * HALF), 2 * HALF)
                        real, imag = [], []
                        for side in range(sides):
                            a_re = buf[side, a, at, re_lanes].astype(jnp.float32)
                            a_im = buf[side, a, at, im_lanes].astype(jnp.float32)
                            b_re = buf[side, b, at, re_lanes].astype(jnp.float32)
                            b_im = buf[side, b, at, im_lanes].astype(jnp.float32)
                            real.append(a_re * b_re + a_im * b_im)
                            imag.append(a_im * b_re - a_re * b_im)
                        acc[lane, z, 0] = sum(real[1:], real[0])
                        acc[lane, z, 1] = sum(imag[1:], imag[0])
                    for part, lanes_at in ((0, re_lanes), (1, im_lanes)):
                        sums = [
                            acc[lane, z, part, pl.ds(0, HALF, 2), :] + acc[lane, z, part, pl.ds(1, HALF, 2), :]
                            for z in range(2)
                        ]
                        out[peer, slot, :, lanes_at] = jnp.concatenate(sums, axis=0).astype(jnp.bfloat16)

        @pl.when(used == 0)
        def _():
            @pl.loop(0, peers)
            def _(peer):
                out[peer, slot] = jnp.zeros((2 * HALF, LENGTH), jnp.bfloat16)


def products(width, info, owns, low, high):
    sides = len(owns)
    return pl.pallas_call(
        lambda *refs: products_kernel(width, sides, *refs),
        out_shape=jax.ShapeDtypeStruct((8 // sides, PCAP, 2 * HALF, LENGTH), jnp.bfloat16),
        in_specs=[SMEM] + [ANY] * (sides + 2),
        out_specs=VMEM,
        scratch_shapes=[
            pltpu.VMEM((sides, BLOCKS + 2 * width, ROWS // sides, LENGTH), jnp.bfloat16),
            pltpu.VMEM((BINS // 128, 2, 2, 2 * HALF, 128), jnp.float32),
            pltpu.SemaphoreType.DMA((sides, 3)),
        ],
        compiler_params=PARAMS,
        cost_estimate=pl.CostEstimate(flops=1 << 25, bytes_accessed=8 << 20, transcendentals=0),
        name="products",
    )(info, *owns, low, high)


def path(records, pairs, owner, width):
    win = lax.axis_index("win")
    far = win // 8
    where = jnp.stack([lax.axis_index("chan"), win % 2]).astype(jnp.int32)
    basis = jnp.asarray(basis_table())
    forward = [(i, i + 1) for i in range(CHAN - 1)]
    backward = [(i + 1, i) for i in range(CHAN - 1)]

    x = records.reshape(BLOCKS, 16, CHUNKS, HALF, 2, LENGTH)
    own, right, left, info = spectra(0, width, where, pairs.T, owner, x, basis)
    low = lax.ppermute(right[None], "chan", forward)
    high = lax.ppermute(left[None], "chan", backward)

    x = records.reshape(BLOCKS, 8, 2, CHUNKS, HALF, 2, LENGTH)
    same, other = split_spectra(1, where, x, basis)
    other = lax.ppermute(other, "win", [(i, i ^ 1) for i in range(16)])
    right, left = lanes(width, info, same, other)
    own, right = lax.optimization_barrier((own, right))
    low_split = lax.ppermute(right, "chan", forward)
    high_split = lax.ppermute(left, "chan", backward)

    chip_groups = [[z * 8 + j for j in range(8)] for z in range(2)]
    core_groups = [[z * 8 + y * 2 + core for y in range(4)] for z in range(2) for core in range(2)]
    far_groups = [[z * 8 + j for z in range(2)] for j in range(8)]

    def near(part):
        total = jnp.sum(part.astype(jnp.float32), axis=0).reshape(PCAP, 2, HALF, LENGTH)
        keep = lax.dynamic_index_in_dim(total, far, axis=1, keepdims=False)
        give = lax.dynamic_index_in_dim(total, 1 - far, axis=1, keepdims=False).astype(jnp.bfloat16)
        return keep, give

    part0 = products(width, info, (own,), low, high)
    part0 = lax.all_to_all(part0, "win", 0, 0, tiled=True, axis_index_groups=chip_groups)
    part1 = products(width, info, (same, other), low_split, high_split)
    part0, _ = lax.optimization_barrier((part0, part1))
    part1 = lax.all_to_all(part1, "win", 0, 0, tiled=True, axis_index_groups=core_groups)
    keep0, give0 = near(part0)
    keep1, give1 = near(part1)
    give = jnp.concatenate([give0, give1], axis=1)
    got = lax.all_gather(give, "win", axis=0, tiled=False, axis_index_groups=far_groups)
    got = lax.dynamic_index_in_dim(got, 1 - far, axis=0, keepdims=False)
    return jnp.concatenate([keep0, keep1], axis=1) + got.astype(jnp.float32), keep0


def local(records, pairs, owner):
    fast, late = path(records, pairs, owner, 2)
    pairs_late, owner_late, _ = lax.optimization_barrier((pairs, owner, late))
    return lax.cond(
        most_needed(pairs_late, owner_late) <= 2,
        lambda fast: fast,
        lambda fast: path(records, pairs, owner, BLOCKS)[0],
        fast,
    )


def solution(mesh):
    return jax.shard_map(
        local,
        mesh=mesh,
        in_specs=(P("chan", None, "win", None), P(), P()),
        out_specs=P("chan", "win", None),
        check_vma=False,
    )
```

```python
import math

import jax
import jax.numpy as jnp
import ml_dtypes
import numpy as np
from jax import lax
from jax.experimental import pallas as pl
from jax.experimental.pallas import tpu as pltpu
from jax.sharding import PartitionSpec as P

PCAP = 4
BLOCKS = 3
CHAN = 32
CHUNKS = 2
LENGTH = 1024
BINS = 512
HALF = 16 // CHUNKS
ROWS = 512 // CHUNKS
VMEM = pl.BlockSpec(memory_space=pltpu.VMEM)
SMEM = pl.BlockSpec(memory_space=pltpu.SMEM)
ANY = pl.BlockSpec(memory_space=pl.ANY)
HBM = pl.BlockSpec(memory_space=pltpu.HBM)
PARAMS = pltpu.CompilerParams(vmem_limit_bytes=40 << 20)
ALL_VMEM = pltpu.CompilerParams(vmem_limit_bytes=63 << 20)


def basis_table():
    sample_ids = np.arange(LENGTH, dtype=np.int32)
    bin_ids = np.arange(BINS, dtype=np.int32)
    step = np.float32(2.0 * math.pi / LENGTH)
    phases = (sample_ids[:, None] * bin_ids[None, :] % LENGTH).astype(np.float32) * step
    taper = np.float32(0.5) - np.float32(0.5) * np.cos(sample_ids.astype(np.float32) * step)
    table = np.concatenate([taper[:, None] * np.cos(phases), -taper[:, None] * np.sin(phases)], axis=1)
    return table.astype(ml_dtypes.bfloat16)


LANES, FIRST, SECOND, USED, TABLE = 0, 6, 10, 14, 18
SWAPS = [
    [pair for low in range(start, CHAN - 1, 2) for pair in ((low, low + 1), (low + 1, low))] for start in (1, 0)
]


def table_kernel(where, pairs_hbm, owner_hbm, narrow, wide, flag, pairs, owner, rows, sems):
    copies = [
        pltpu.make_async_copy(pairs_hbm, pairs, sems.at[0]),
        pltpu.make_async_copy(owner_hbm, owner, sems.at[1]),
    ]
    for copy in copies:
        copy.start()
    odd = where[0] % 2
    me = where[0].astype(jnp.float32)
    count = owner.shape[1]
    for copy in copies:
        copy.wait()
    rows[...] = jnp.full(rows.shape, -1000.0, jnp.float32)
    rows[0:2, 0:count] = pairs[...].astype(jnp.float32)
    rows[2:3, 0:count] = owner[...].astype(jnp.float32)
    first = rows[0:1, :]
    second = rows[1:2, :]
    holder = rows[2:3, :]

    chan = lax.broadcasted_iota(jnp.int32, (CHAN, 128), 0).astype(jnp.float32)

    def all_three(block, step):
        hits = [
            jnp.max(jnp.where((block == BLOCKS * chan + i) & (holder == chan + step), 1.0, 0.0), axis=1, keepdims=True)
            for i in range(BLOCKS)
        ]
        return hits[0] * hits[1] * hits[2]

    most = jnp.max(jnp.maximum(all_three(first, 1.0), all_three(second, -1.0)))

    def total(hit, value=1.0):
        return jnp.sum(jnp.where(hit, value, 0.0))

    first = first - BLOCKS * me
    second = second - BLOCKS * me
    apart = holder - me
    mine = apart == 0.0

    def needs(hit, block):
        return [(total(hit & (block == float(i))) > 0.0).astype(jnp.int32) for i in range(BLOCKS)]

    to_right = needs(apart == 1.0, first)
    to_left = needs(apart == -1.0, second)
    of_left = needs(mine, first + BLOCKS)
    of_right = needs(mine, second - BLOCKS)
    earlier = lax.broadcasted_iota(jnp.int32, (128, 128), 0) < lax.broadcasted_iota(jnp.int32, (128, 128), 1)
    ranks = jnp.dot(
        jnp.broadcast_to(jnp.where(mine, 1.0, 0.0), (8, 128)).astype(jnp.bfloat16),
        jnp.where(earlier, 1.0, 0.0).astype(jnp.bfloat16),
        preferred_element_type=jnp.float32,
    )[0:1, :]
    number = total(mine).astype(jnp.int32)

    def spot(need, block, width):
        if width == BLOCKS:
            return block
        return jnp.where(block == 0, 0, jnp.where(block == 1, need[0], jnp.minimum(need[0] + need[1], width - 1)))

    def picks(need, width):
        if width == BLOCKS:
            return [jnp.int32(i) for i in range(BLOCKS)]
        n0, n1, n2 = [n > 0 for n in need]
        lowest = jnp.where(n0, 0, jnp.where(n1, 1, jnp.where(n2, 2, 0)))
        after = jnp.where(n0 & n1, 1, jnp.where(n2 & (n0 | n1), 2, 0))
        return [lowest.astype(jnp.int32), after.astype(jnp.int32), jnp.int32(0)]

    flag[0] = most.astype(jnp.int32)
    for info, width in ((narrow, 2), (wide, BLOCKS)):
        for i, (right, left) in enumerate(zip(picks(to_right, width), picks(to_left, width))):
            info[LANES + i] = jnp.where(odd == 1, right, left)
            info[LANES + 3 + i] = jnp.where(odd == 1, left, right)
    for slot in range(PCAP):
        hit = mine & (ranks == float(slot))
        a = total(hit, first).astype(jnp.int32)
        b = total(hit, second).astype(jnp.int32)
        used = (number > slot).astype(jnp.int32)
        for info, width in ((narrow, 2), (wide, BLOCKS)):
            from_left = BLOCKS + odd * width
            from_right = BLOCKS + (1 - odd) * width
            info[FIRST + slot] = jnp.where(a < 0, from_left + spot(of_left, a + BLOCKS, width), a)
            info[SECOND + slot] = jnp.where(b >= BLOCKS, from_right + spot(of_right, b - BLOCKS, width), b)
            info[USED + slot] = used


def tables(where, pairs, owner):
    table = jax.ShapeDtypeStruct((TABLE,), jnp.int32)
    return pl.pallas_call(
        table_kernel,
        out_shape=(table, table, jax.ShapeDtypeStruct((1,), jnp.int32)),
        in_specs=[SMEM, HBM, HBM],
        out_specs=[SMEM] * 3,
        scratch_shapes=[
            pltpu.VMEM((2, pairs.shape[0]), jnp.int32),
            pltpu.VMEM((1, pairs.shape[0]), jnp.int32),
            pltpu.VMEM((8, 128), jnp.float32),
            pltpu.SemaphoreType.DMA((2,)),
        ],
        compiler_params=ALL_VMEM,
        name="tables",
    )(where, pairs.T, owner[None])


def whitened(rows, basis):
    spectrum = jnp.dot(rows, basis, preferred_element_type=jnp.float32)
    power_mean = jnp.mean(spectrum * spectrum, axis=-1, keepdims=True)
    return (spectrum * lax.rsqrt(power_mean + 1e-06)).astype(jnp.bfloat16)


COST = pl.CostEstimate(flops=2 * 3 * ROWS * LENGTH * LENGTH, bytes_accessed=8 << 20, transcendentals=0)


def deal_kernel(x, deal, buf, xsem, dsem):
    loads = [pltpu.make_async_copy(x.at[block, :, 1], buf.at[block], xsem.at[block]) for block in range(BLOCKS)]
    stores = [
        [
            pltpu.make_async_copy(buf.at[block, z * 8 + peer], deal.at[peer, block, z], dsem.at[peer, block, z])
            for peer in range(8)
            for z in range(2)
        ]
        for block in range(BLOCKS)
    ]
    for copy in loads:
        copy.start()
    for load, copies in zip(loads, stores):
        load.wait()
        for copy in copies:
            copy.start()
    for copies in stores:
        for copy in copies:
            copy.wait()


def dealing(x):
    return pl.pallas_call(
        deal_kernel,
        out_shape=jax.ShapeDtypeStruct((8, BLOCKS, 2, HALF, 2, LENGTH), jnp.bfloat16),
        in_specs=[HBM],
        out_specs=ANY,
        scratch_shapes=[
            pltpu.VMEM((BLOCKS, 16, HALF, 2, LENGTH), jnp.bfloat16),
            pltpu.SemaphoreType.DMA((BLOCKS,)),
            pltpu.SemaphoreType.DMA((8, BLOCKS, 2)),
        ],
        compiler_params=PARAMS,
        cost_estimate=pl.CostEstimate(flops=0, bytes_accessed=3 << 20, transcendentals=0),
        name="deal",
    )(x)


def lane_copy(buf, block, lanes, way, spot, lsem):
    return pltpu.make_async_copy(buf.at[block], lanes[way].at[spot], lsem.at[way, spot])


def start_lanes(width, info, buf, block, lanes, lsem):
    for way in range(2):
        for spot in range(width):

            @pl.when(info[LANES + way * 3 + spot] == block)
            def _(way=way, spot=spot):
                lane_copy(buf, block, lanes, way, spot, lsem).start()


def wait_lanes(width, buf, lanes, lsem):
    for way in range(2):
        for spot in range(width):
            lane_copy(buf, 0, lanes, way, spot, lsem).wait()


def raw_lanes_kernel(width, info, x, one, two, buf, xsem, lsem):
    loads = [pltpu.make_async_copy(x.at[block, :, 0], buf.at[block], xsem.at[block]) for block in range(BLOCKS)]
    for copy in loads:
        copy.start()
    for block, copy in enumerate(loads):
        copy.wait()
        start_lanes(width, info, buf, block, (one, two), lsem)
    wait_lanes(width, buf, (one, two), lsem)


def raw_lanes(width, info, x):
    lane = jax.ShapeDtypeStruct((width, 16, HALF, 2, LENGTH), jnp.bfloat16)
    return pl.pallas_call(
        lambda *refs: raw_lanes_kernel(width, *refs),
        out_shape=(lane, lane),
        in_specs=[SMEM, HBM],
        out_specs=[ANY] * 2,
        scratch_shapes=[
            pltpu.VMEM((BLOCKS, 16, HALF, 2, LENGTH), jnp.bfloat16),
            pltpu.SemaphoreType.DMA((BLOCKS,)),
            pltpu.SemaphoreType.DMA((2, width)),
        ],
        compiler_params=PARAMS,
        cost_estimate=pl.CostEstimate(flops=0, bytes_accessed=4 << 20, transcendentals=0),
        name="raw_lanes",
    )(info, x)


def spectra_kernel(count, at, x, basis, own, xbuf, spec, xsem, osem):
    def load(block):
        return pltpu.make_async_copy(x.at[at(block)], xbuf.at[block], xsem.at[block])

    def store(block):
        return pltpu.make_async_copy(spec.at[block], own.at[block], osem.at[block])

    for block in range(count):
        load(block).start()
    for block in range(count):
        load(block).wait()
        spec[block] = whitened(xbuf[block].reshape(ROWS, LENGTH), basis[...])
        store(block).start()
    for block in range(count):
        store(block).wait()


def spectra(count, at, x, basis):
    return pl.pallas_call(
        lambda *refs: spectra_kernel(count, at, *refs),
        out_shape=jax.ShapeDtypeStruct((count, ROWS, LENGTH), jnp.bfloat16),
        in_specs=[HBM, VMEM],
        out_specs=ANY,
        scratch_shapes=[
            pltpu.VMEM((count, 16, HALF, 2, LENGTH), jnp.bfloat16),
            pltpu.VMEM((count, ROWS, LENGTH), jnp.bfloat16),
            pltpu.SemaphoreType.DMA((count,)),
            pltpu.SemaphoreType.DMA((count,)),
        ],
        compiler_params=PARAMS,
        cost_estimate=COST,
        name="spectra",
    )(x, basis)


def dealt_kernel(width, info, x, basis, own, one, two, spec, osem, lsem):
    def store(block):
        return pltpu.make_async_copy(spec.at[block], own.at[block], osem.at[block])

    for block in range(BLOCKS):
        spec[block] = whitened(x[:, block].reshape(ROWS, LENGTH), basis[...])
        start_lanes(width, info, spec, block, (one, two), lsem)
        store(block).start()
    wait_lanes(width, spec, (one, two), lsem)
    for block in range(BLOCKS):
        store(block).wait()


def dealt_spectra(width, info, x, basis):
    own = jax.ShapeDtypeStruct((BLOCKS, ROWS, LENGTH), jnp.bfloat16)
    lane = jax.ShapeDtypeStruct((width, ROWS, LENGTH), jnp.bfloat16)
    return pl.pallas_call(
        lambda *refs: dealt_kernel(width, *refs),
        out_shape=(own, lane, lane),
        in_specs=[SMEM, VMEM, VMEM],
        out_specs=[HBM] * 3,
        scratch_shapes=[
            pltpu.VMEM((BLOCKS, ROWS, LENGTH), jnp.bfloat16),
            pltpu.SemaphoreType.DMA((BLOCKS,)),
            pltpu.SemaphoreType.DMA((2, width)),
        ],
        compiler_params=PARAMS,
        cost_estimate=COST,
        name="dealt_spectra",
    )(info, x, basis)


def parts(read, at, lane):
    a_re, a_im, b_re, b_im = [
        read(operand, at, pl.ds(start + lane * 128, 128)).astype(jnp.float32)
        for operand in range(2)
        for start in (0, BINS)
    ]
    return a_re * b_re + a_im * b_im, a_im * b_re - a_re * b_im


def pair_sums(acc):
    return acc[pl.ds(0, HALF, 2), :] + acc[pl.ds(1, HALF, 2), :]


def tile(index):
    return pl.ds(pl.multiple_of(index * 2 * HALF, 2 * HALF), 2 * HALF)


def raw_products_kernel(width, info, basis, own, one, two, out, xbuf, buf, acc, xsem, osem):
    loads = [pltpu.make_async_copy(two.at[spot], xbuf.at[spot], xsem.at[spot]) for spot in range(width)]
    ready = [
        pltpu.make_async_copy(own, buf.at[pl.ds(0, BLOCKS)], osem.at[0]),
        pltpu.make_async_copy(one, buf.at[pl.ds(BLOCKS, width)], osem.at[1]),
    ]
    for copy in loads + ready:
        copy.start()
    for spot, copy in enumerate(loads):
        copy.wait()
        buf[BLOCKS + width + spot] = whitened(xbuf[spot].reshape(ROWS, LENGTH), basis[...])
    for copy in ready:
        copy.wait()

    @pl.loop(0, PCAP)
    def _(slot):
        spots = info[FIRST + slot], info[SECOND + slot]

        def read(operand, at, part):
            return buf[spots[operand], at, part]

        @pl.when(info[USED + slot] > 0)
        def _():
            @pl.loop(0, 8)
            def _(peer):
                for lane in range(BINS // 128):
                    for z in range(2):
                        acc[lane, z, 0], acc[lane, z, 1] = parts(read, tile(z * 8 + peer), lane)
                    for part in range(2):
                        sums = [pair_sums(acc.at[lane, z, part]) for z in range(2)]
                        out[peer, slot, :, pl.ds(part * BINS + lane * 128, 128)] = jnp.concatenate(
                            sums, axis=0
                        ).astype(jnp.bfloat16)

        @pl.when(info[USED + slot] == 0)
        def _():
            @pl.loop(0, 8)
            def _(peer):
                out[peer, slot] = jnp.zeros((2 * HALF, LENGTH), jnp.bfloat16)


def raw_products(width, info, basis, own, one, two):
    return pl.pallas_call(
        lambda *refs: raw_products_kernel(width, *refs),
        out_shape=jax.ShapeDtypeStruct((8, PCAP, 2 * HALF, LENGTH), jnp.bfloat16),
        in_specs=[SMEM, VMEM, ANY, ANY, HBM],
        out_specs=VMEM,
        scratch_shapes=[
            pltpu.VMEM((width, 16, HALF, 2, LENGTH), jnp.bfloat16),
            pltpu.VMEM((BLOCKS + 2 * width, ROWS, LENGTH), jnp.bfloat16),
            pltpu.VMEM((BINS // 128, 2, 2, 2 * HALF, 128), jnp.float32),
            pltpu.SemaphoreType.DMA((width,)),
            pltpu.SemaphoreType.DMA((2,)),
        ],
        compiler_params=PARAMS,
        cost_estimate=COST,
        name="raw_products",
    )(info, basis, own, one, two)


def dealt_products_kernel(width, info, own, one, two, out, buf, acc, sems):
    def start(slot, operand, spot):
        to, sem = buf.at[slot, operand], sems.at[slot, operand]

        @pl.when(spot < BLOCKS)
        def _():
            pltpu.make_async_copy(own.at[spot], to, sem).start()

        @pl.when((spot >= BLOCKS) & (spot < BLOCKS + width))
        def _():
            pltpu.make_async_copy(one.at[spot - BLOCKS], to, sem).start()

        @pl.when(spot >= BLOCKS + width)
        def _():
            pltpu.make_async_copy(two.at[spot - BLOCKS - width], to, sem).start()

    for slot in range(PCAP):

        @pl.when(info[USED + slot] > 0)
        def _(slot=slot):
            start(slot, 0, info[FIRST + slot])
            start(slot, 1, info[SECOND + slot])

    @pl.loop(0, PCAP)
    def _(slot):
        def read(operand, at, part):
            return buf[slot, operand, at, part]

        @pl.when(info[USED + slot] > 0)
        def _():
            for operand in range(2):
                pltpu.make_async_copy(own.at[0], buf.at[slot, operand], sems.at[slot, operand]).wait()

            @pl.loop(0, 2)
            def _(z):
                for lane in range(BINS // 128):
                    real, imag = parts(read, tile(z), lane)
                    for source in range(1, 8):
                        re, im = parts(read, tile(source * 2 + z), lane)
                        real, imag = real + re, imag + im
                    acc[lane, 0], acc[lane, 1] = real, imag
                    for part in range(2):
                        out[z, slot, :, pl.ds(part * BINS + lane * 128, 128)] = pair_sums(acc.at[lane, part])

        @pl.when(info[USED + slot] == 0)
        def _():
            for z in range(2):
                out[z, slot] = jnp.zeros((HALF, LENGTH), jnp.float32)


def dealt_products(width, info, own, one, two):
    return pl.pallas_call(
        lambda *refs: dealt_products_kernel(width, *refs),
        out_shape=jax.ShapeDtypeStruct((2, PCAP, HALF, LENGTH), jnp.float32),
        in_specs=[SMEM] + [ANY] * 3,
        out_specs=VMEM,
        scratch_shapes=[
            pltpu.VMEM((PCAP, 2, ROWS, LENGTH), jnp.bfloat16),
            pltpu.VMEM((BINS // 128, 2, 2 * HALF, 128), jnp.float32),
            pltpu.SemaphoreType.DMA((PCAP, 2)),
        ],
        compiler_params=PARAMS,
        cost_estimate=pl.CostEstimate(flops=1 << 25, bytes_accessed=8 << 20, transcendentals=0),
        name="dealt_products",
    )(info, own, one, two)


def path(records, info, width):
    far = lax.axis_index("win") // 8
    basis = jnp.asarray(basis_table())
    x = records.reshape(BLOCKS, 16, CHUNKS, HALF, 2, LENGTH)
    chip_groups = [[z * 8 + j for j in range(8)] for z in range(2)]
    far_groups = [[z * 8 + j for z in range(2)] for j in range(8)]

    deal = dealing(x)
    x, deal = lax.optimization_barrier((x, deal))
    dealt = lax.all_to_all(deal, "win", 0, 0, tiled=True, axis_index_groups=chip_groups)
    raw_one, raw_two = [lax.ppermute(lane, "chan", swap) for lane, swap in zip(raw_lanes(width, info, x), SWAPS)]
    dealt_own, *sent = dealt_spectra(width, info, dealt, basis)
    raw_basis, *sent = lax.optimization_barrier((basis, *sent))
    came = [lax.ppermute(lane, "chan", swap) for lane, swap in zip(sent, SWAPS)]
    own = spectra(BLOCKS, lambda block: (block, slice(None), 0), x, basis)
    one = spectra(width, lambda spot: (spot,), raw_one, raw_basis)

    part = raw_products(width, info, raw_basis, own, one, raw_two)
    first = lax.all_to_all(part, "win", 0, 0, tiled=True, axis_index_groups=chip_groups)
    dealt_own, part = lax.optimization_barrier((dealt_own, part))
    second = dealt_products(width, info, dealt_own, *came)
    first, second = lax.optimization_barrier((first, second))
    first = jnp.sum(first.astype(jnp.float32), axis=0).reshape(PCAP, 2, HALF, LENGTH)

    def half(at):
        return jnp.concatenate(
            [
                lax.dynamic_index_in_dim(first, at, axis=1, keepdims=False),
                lax.dynamic_index_in_dim(second, at, axis=0, keepdims=False),
            ],
            axis=1,
        )

    give = half(1 - far).astype(jnp.bfloat16)

    def swapped(slots):
        got = lax.all_gather(give[:slots], "win", axis=0, tiled=True, axis_index_groups=far_groups)
        got = lax.dynamic_slice_in_dim(got, (1 - far) * slots, slots, axis=0).astype(jnp.float32)
        return jnp.concatenate([got, jnp.zeros((PCAP - slots,) + got.shape[1:], jnp.float32)], axis=0)

    got = lax.cond(info[USED + 2] > 0, lambda: swapped(PCAP), lambda: swapped(PCAP // 2))
    return half(far) + got


def local(records, pairs, owner):
    where = lax.axis_index("chan")[None].astype(jnp.int32)
    narrow, wide, three = tables(where, pairs, owner)
    return lax.cond(
        three.reshape(()) == 0,
        lambda: path(records, narrow, 2),
        lambda: path(records, wide, BLOCKS),
    )


def solution(mesh):
    return jax.shard_map(
        local,
        mesh=mesh,
        in_specs=(P("chan", None, "win", None), P(), P()),
        out_specs=P("chan", "win", None),
        check_vma=False,
    )
```

```python
import math

import jax
import jax.numpy as jnp
import ml_dtypes
import numpy as np
from jax import lax
from jax.experimental import pallas as pl
from jax.experimental.pallas import tpu as pltpu
from jax.sharding import PartitionSpec as P

PCAP = 4
BLOCKS = 3
CHAN = 32
CHUNKS = 2
LENGTH = 1024
BINS = 512
HALF = 16 // CHUNKS
ROWS = 512 // CHUNKS
VMEM = pl.BlockSpec(memory_space=pltpu.VMEM)
SMEM = pl.BlockSpec(memory_space=pltpu.SMEM)
ANY = pl.BlockSpec(memory_space=pl.ANY)
HBM = pl.BlockSpec(memory_space=pltpu.HBM)
PARAMS = pltpu.CompilerParams(vmem_limit_bytes=40 << 20)
ALL_VMEM = pltpu.CompilerParams(vmem_limit_bytes=63 << 20)


def basis_table():
    sample_ids = np.arange(LENGTH, dtype=np.int32)
    bin_ids = np.arange(BINS, dtype=np.int32)
    step = np.float32(2.0 * math.pi / LENGTH)
    phases = (sample_ids[:, None] * bin_ids[None, :] % LENGTH).astype(np.float32) * step
    taper = np.float32(0.5) - np.float32(0.5) * np.cos(sample_ids.astype(np.float32) * step)
    table = np.concatenate([taper[:, None] * np.cos(phases), -taper[:, None] * np.sin(phases)], axis=1)
    return table.astype(ml_dtypes.bfloat16)


LANES, FIRST, SECOND, USED, TABLE = 0, 6, 10, 14, 18
SWAPS = [
    [pair for low in range(start, CHAN - 1, 2) for pair in ((low, low + 1), (low + 1, low))] for start in (1, 0)
]


def fill_tables(where, pairs_hbm, owner_hbm, narrow, wide, flag, pairs, owner, rows, sems):
    copies = [
        pltpu.make_async_copy(pairs_hbm, pairs, sems.at[0]),
        pltpu.make_async_copy(owner_hbm, owner, sems.at[1]),
    ]
    for copy in copies:
        copy.start()
    odd = where[0] % 2
    me = where[0].astype(jnp.float32)
    count = owner.shape[1]
    for copy in copies:
        copy.wait()
    rows[...] = jnp.full(rows.shape, -1000.0, jnp.float32)
    rows[0:2, 0:count] = pairs[...].astype(jnp.float32)
    rows[2:3, 0:count] = owner[...].astype(jnp.float32)
    first = rows[0:1, :]
    second = rows[1:2, :]
    holder = rows[2:3, :]

    chan = lax.broadcasted_iota(jnp.int32, (CHAN, 128), 0).astype(jnp.float32)

    def all_three(block, step):
        hits = [
            jnp.max(jnp.where((block == BLOCKS * chan + i) & (holder == chan + step), 1.0, 0.0), axis=1, keepdims=True)
            for i in range(BLOCKS)
        ]
        return hits[0] * hits[1] * hits[2]

    most = jnp.max(jnp.maximum(all_three(first, 1.0), all_three(second, -1.0)))

    def total(hit, value=1.0):
        return jnp.sum(jnp.where(hit, value, 0.0))

    first = first - BLOCKS * me
    second = second - BLOCKS * me
    apart = holder - me
    mine = apart == 0.0

    def needs(hit, block):
        return [(total(hit & (block == float(i))) > 0.0).astype(jnp.int32) for i in range(BLOCKS)]

    to_right = needs(apart == 1.0, first)
    to_left = needs(apart == -1.0, second)
    of_left = needs(mine, first + BLOCKS)
    of_right = needs(mine, second - BLOCKS)
    earlier = lax.broadcasted_iota(jnp.int32, (128, 128), 0) < lax.broadcasted_iota(jnp.int32, (128, 128), 1)
    ranks = jnp.dot(
        jnp.broadcast_to(jnp.where(mine, 1.0, 0.0), (8, 128)).astype(jnp.bfloat16),
        jnp.where(earlier, 1.0, 0.0).astype(jnp.bfloat16),
        preferred_element_type=jnp.float32,
    )[0:1, :]
    number = total(mine).astype(jnp.int32)

    def spot(need, block, width):
        if width == BLOCKS:
            return block
        return jnp.where(block == 0, 0, jnp.where(block == 1, need[0], jnp.minimum(need[0] + need[1], width - 1)))

    def picks(need, width):
        if width == BLOCKS:
            return [jnp.int32(i) for i in range(BLOCKS)]
        n0, n1, n2 = [n > 0 for n in need]
        lowest = jnp.where(n0, 0, jnp.where(n1, 1, jnp.where(n2, 2, 0)))
        after = jnp.where(n0 & n1, 1, jnp.where(n2 & (n0 | n1), 2, lowest))
        return [lowest.astype(jnp.int32), after.astype(jnp.int32), jnp.int32(0)]

    flag[0] = most.astype(jnp.int32)
    for info, width in ((narrow, 2), (wide, BLOCKS)):
        for i, (right, left) in enumerate(zip(picks(to_right, width), picks(to_left, width))):
            info[LANES + i] = jnp.where(odd == 1, right, left)
            info[LANES + 3 + i] = jnp.where(odd == 1, left, right)
    for slot in range(PCAP):
        hit = mine & (ranks == float(slot))
        a = total(hit, first).astype(jnp.int32)
        b = total(hit, second).astype(jnp.int32)
        used = (number > slot).astype(jnp.int32)
        for info, width in ((narrow, 2), (wide, BLOCKS)):
            from_left = BLOCKS + odd * width
            from_right = BLOCKS + (1 - odd) * width
            info[FIRST + slot] = jnp.where(a < 0, from_left + spot(of_left, a + BLOCKS, width), a)
            info[SECOND + slot] = jnp.where(b >= BLOCKS, from_right + spot(of_right, b - BLOCKS, width), b)
            info[USED + slot] = used


def whitened(rows, basis):
    spectrum = jnp.dot(rows, basis, preferred_element_type=jnp.float32)
    power_mean = jnp.mean(spectrum * spectrum, axis=-1, keepdims=True)
    return (spectrum * lax.rsqrt(power_mean + 1e-06)).astype(jnp.bfloat16)


COST = pl.CostEstimate(flops=2 * 3 * ROWS * LENGTH * LENGTH, bytes_accessed=8 << 20, transcendentals=0)


def lane_copy(buf, block, lanes, way, spot, lsem):
    return pltpu.make_async_copy(buf.at[block], lanes[way].at[spot], lsem.at[way, spot])


def start_lanes(width, info, buf, block, lanes, lsem):
    for way in range(2):
        for spot in range(width):

            @pl.when(info[LANES + way * 3 + spot] == block)
            def _(way=way, spot=spot):
                lane_copy(buf, block, lanes, way, spot, lsem).start()


def wait_lanes(width, buf, lanes, lsem):
    for way in range(2):
        for spot in range(width):
            lane_copy(buf, 0, lanes, way, spot, lsem).wait()


def raw_lanes_kernel(width, info, x, one, two, buf, xsem, lsem):
    loads = [pltpu.make_async_copy(x.at[block, :, 0], buf.at[block], xsem.at[block]) for block in range(BLOCKS)]
    for copy in loads:
        copy.start()
    for block, copy in enumerate(loads):
        copy.wait()
        start_lanes(width, info, buf, block, (one, two), lsem)
    wait_lanes(width, buf, (one, two), lsem)


def raw_lanes(width, info, x):
    lane = jax.ShapeDtypeStruct((width, 16, HALF, 2, LENGTH), jnp.bfloat16)
    return pl.pallas_call(
        lambda *refs: raw_lanes_kernel(width, *refs),
        out_shape=(lane, lane),
        in_specs=[SMEM, HBM],
        out_specs=[ANY] * 2,
        scratch_shapes=[
            pltpu.VMEM((BLOCKS, 16, HALF, 2, LENGTH), jnp.bfloat16),
            pltpu.SemaphoreType.DMA((BLOCKS,)),
            pltpu.SemaphoreType.DMA((2, width)),
        ],
        compiler_params=PARAMS,
        cost_estimate=pl.CostEstimate(flops=0, bytes_accessed=4 << 20, transcendentals=0),
        name="raw_lanes",
    )(info, x)


def prepare_kernel(where, pairs, owner, x, narrow, wide, flag, deal, one, two, *scratch):
    small, (buf, xsem, dsem, lsem) = scratch[:4], scratch[4:]
    loads = [
        [pltpu.make_async_copy(x.at[block, :, chunk], buf.at[chunk, block], xsem.at[chunk, block]) for block in range(BLOCKS)]
        for chunk in range(CHUNKS)
    ]
    for copies in reversed(loads):
        for copy in copies:
            copy.start()
    fill_tables(where, pairs, owner, narrow, wide, flag, *small)
    deals = [
        [
            pltpu.make_async_copy(buf.at[1, block, z * 8 + peer], deal.at[peer, block, z], dsem.at[peer, block, z])
            for peer in range(8)
            for z in range(2)
        ]
        for block in range(BLOCKS)
    ]
    for block in range(BLOCKS):
        loads[1][block].wait()
        for copy in deals[block]:
            copy.start()
    for block in range(BLOCKS):
        loads[0][block].wait()
        start_lanes(2, narrow, buf.at[0], block, (one, two), lsem)
    for copies in deals:
        for copy in copies:
            copy.wait()
    wait_lanes(2, buf.at[0], (one, two), lsem)


def prepare(where, pairs, owner, x):
    table = jax.ShapeDtypeStruct((TABLE,), jnp.int32)
    lane = jax.ShapeDtypeStruct((2, 16, HALF, 2, LENGTH), jnp.bfloat16)
    return pl.pallas_call(
        prepare_kernel,
        out_shape=(
            table,
            table,
            jax.ShapeDtypeStruct((1,), jnp.int32),
            jax.ShapeDtypeStruct((8, BLOCKS, 2, HALF, 2, LENGTH), jnp.bfloat16),
            lane,
            lane,
        ),
        in_specs=[SMEM, HBM, HBM, HBM],
        out_specs=[SMEM] * 3 + [ANY] * 3,
        scratch_shapes=[
            pltpu.VMEM((2, pairs.shape[0]), jnp.int32),
            pltpu.VMEM((1, pairs.shape[0]), jnp.int32),
            pltpu.VMEM((8, 128), jnp.float32),
            pltpu.SemaphoreType.DMA((2,)),
            pltpu.VMEM((CHUNKS, BLOCKS, 16, HALF, 2, LENGTH), jnp.bfloat16),
            pltpu.SemaphoreType.DMA((CHUNKS, BLOCKS)),
            pltpu.SemaphoreType.DMA((8, BLOCKS, 2)),
            pltpu.SemaphoreType.DMA((2, 2)),
        ],
        compiler_params=ALL_VMEM,
        cost_estimate=pl.CostEstimate(flops=0, bytes_accessed=7 << 20, transcendentals=0),
        name="prepare",
    )(where, pairs.T, owner[None], x)


def spectra_kernel(count, at, x, basis, own, xbuf, spec, xsem, osem):
    def load(block):
        return pltpu.make_async_copy(x.at[at(block)], xbuf.at[block], xsem.at[block])

    def store(block):
        return pltpu.make_async_copy(spec.at[block], own.at[block], osem.at[block])

    for block in range(count):
        load(block).start()
    for block in range(count):
        load(block).wait()
        spec[block] = whitened(xbuf[block].reshape(ROWS, LENGTH), basis[...])
        store(block).start()
    for block in range(count):
        store(block).wait()


def spectra(count, at, x, basis):
    return pl.pallas_call(
        lambda *refs: spectra_kernel(count, at, *refs),
        out_shape=jax.ShapeDtypeStruct((count, ROWS, LENGTH), jnp.bfloat16),
        in_specs=[HBM, VMEM],
        out_specs=ANY,
        scratch_shapes=[
            pltpu.VMEM((count, 16, HALF, 2, LENGTH), jnp.bfloat16),
            pltpu.VMEM((count, ROWS, LENGTH), jnp.bfloat16),
            pltpu.SemaphoreType.DMA((count,)),
            pltpu.SemaphoreType.DMA((count,)),
        ],
        compiler_params=PARAMS,
        cost_estimate=COST,
        name="spectra",
    )(x, basis)


def dealt_kernel(width, info, x, basis, one, two, spec, lsem):
    for block in range(BLOCKS):
        picks = [info[LANES + way * 3 + spot] == block for way in range(2) for spot in range(width)]
        wanted = picks[0]
        for pick in picks[1:]:
            wanted = wanted | pick

        @pl.when(wanted)
        def _(block=block):
            spec[block] = whitened(x[:, block].reshape(ROWS, LENGTH), basis[...])
            start_lanes(width, info, spec, block, (one, two), lsem)

    wait_lanes(width, spec, (one, two), lsem)


def dealt_lanes(width, info, x, basis):
    lane = jax.ShapeDtypeStruct((width, ROWS, LENGTH), jnp.bfloat16)
    return pl.pallas_call(
        lambda *refs: dealt_kernel(width, *refs),
        out_shape=(lane, lane),
        in_specs=[SMEM, VMEM, VMEM],
        out_specs=[HBM] * 2,
        scratch_shapes=[
            pltpu.VMEM((BLOCKS, ROWS, LENGTH), jnp.bfloat16),
            pltpu.SemaphoreType.DMA((2, width)),
        ],
        compiler_params=PARAMS,
        cost_estimate=COST,
        name="dealt_lanes",
    )(info, x, basis)


def dealt_own_kernel(x, basis, own):
    for block in range(BLOCKS):
        own[block] = whitened(x[:, block].reshape(ROWS, LENGTH), basis[...])


def dealt_spectra(x, basis):
    return pl.pallas_call(
        dealt_own_kernel,
        out_shape=jax.ShapeDtypeStruct((BLOCKS, ROWS, LENGTH), jnp.bfloat16),
        in_specs=[VMEM, VMEM],
        out_specs=VMEM,
        compiler_params=PARAMS,
        cost_estimate=COST,
        name="dealt_spectra",
    )(x, basis)


def parts(read, at, lane):
    a_re, a_im, b_re, b_im = [
        read(operand, at, pl.ds(start + lane * 128, 128)).astype(jnp.float32)
        for operand in range(2)
        for start in (0, BINS)
    ]
    return a_re * b_re + a_im * b_im, a_im * b_re - a_re * b_im


def pair_sums(acc):
    return acc[pl.ds(0, HALF, 2), :] + acc[pl.ds(1, HALF, 2), :]


def tile(index):
    return pl.ds(pl.multiple_of(index * 2 * HALF, 2 * HALF), 2 * HALF)


def raw_products_kernel(width, info, basis, own, one, two, out, xbuf, buf, acc, xsem, osem):
    loads = [pltpu.make_async_copy(two.at[spot], xbuf.at[spot], xsem.at[spot]) for spot in range(width)]
    ready = [
        pltpu.make_async_copy(own, buf.at[pl.ds(0, BLOCKS)], osem.at[0]),
        pltpu.make_async_copy(one, buf.at[pl.ds(BLOCKS, width)], osem.at[1]),
    ]
    for copy in loads + ready:
        copy.start()
    for spot, copy in enumerate(loads):
        copy.wait()
        buf[BLOCKS + width + spot] = whitened(xbuf[spot].reshape(ROWS, LENGTH), basis[...])
    for copy in ready:
        copy.wait()

    @pl.loop(0, PCAP)
    def _(slot):
        spots = info[FIRST + slot], info[SECOND + slot]

        def read(operand, at, part):
            return buf[spots[operand], at, part]

        @pl.when(info[USED + slot] > 0)
        def _():
            @pl.loop(0, 8)
            def _(peer):
                for lane in range(BINS // 128):
                    for z in range(2):
                        acc[lane, z, 0], acc[lane, z, 1] = parts(read, tile(z * 8 + peer), lane)
                    for part in range(2):
                        sums = [pair_sums(acc.at[lane, z, part]) for z in range(2)]
                        out[peer, slot, :, pl.ds(part * BINS + lane * 128, 128)] = jnp.concatenate(
                            sums, axis=0
                        ).astype(jnp.bfloat16)

        @pl.when(info[USED + slot] == 0)
        def _():
            @pl.loop(0, 8)
            def _(peer):
                out[peer, slot] = jnp.zeros((2 * HALF, LENGTH), jnp.bfloat16)


def raw_products(width, info, basis, own, one, two):
    return pl.pallas_call(
        lambda *refs: raw_products_kernel(width, *refs),
        out_shape=jax.ShapeDtypeStruct((8, PCAP, 2 * HALF, LENGTH), jnp.bfloat16),
        in_specs=[SMEM, VMEM, ANY, ANY, HBM],
        out_specs=VMEM,
        scratch_shapes=[
            pltpu.VMEM((width, 16, HALF, 2, LENGTH), jnp.bfloat16),
            pltpu.VMEM((BLOCKS + 2 * width, ROWS, LENGTH), jnp.bfloat16),
            pltpu.VMEM((BINS // 128, 2, 2, 2 * HALF, 128), jnp.float32),
            pltpu.SemaphoreType.DMA((width,)),
            pltpu.SemaphoreType.DMA((2,)),
        ],
        compiler_params=PARAMS,
        cost_estimate=COST,
        name="raw_products",
    )(info, basis, own, one, two)


def dealt_products_kernel(width, info, own, one, two, out, buf, acc, sems):
    def start(slot, operand, spot):
        to, sem = buf.at[slot, operand], sems.at[slot, operand]

        @pl.when(spot < BLOCKS)
        def _():
            pltpu.make_async_copy(own.at[spot], to, sem).start()

        @pl.when((spot >= BLOCKS) & (spot < BLOCKS + width))
        def _():
            pltpu.make_async_copy(one.at[spot - BLOCKS], to, sem).start()

        @pl.when(spot >= BLOCKS + width)
        def _():
            pltpu.make_async_copy(two.at[spot - BLOCKS - width], to, sem).start()

    for slot in range(PCAP):

        @pl.when(info[USED + slot] > 0)
        def _(slot=slot):
            start(slot, 0, info[FIRST + slot])
            start(slot, 1, info[SECOND + slot])

    @pl.loop(0, PCAP)
    def _(slot):
        def read(operand, at, part):
            return buf[slot, operand, at, part]

        @pl.when(info[USED + slot] > 0)
        def _():
            for operand in range(2):
                pltpu.make_async_copy(own.at[0], buf.at[slot, operand], sems.at[slot, operand]).wait()

            @pl.loop(0, 2)
            def _(z):
                for lane in range(BINS // 128):
                    real, imag = parts(read, tile(z), lane)
                    for source in range(1, 8):
                        re, im = parts(read, tile(source * 2 + z), lane)
                        real, imag = real + re, imag + im
                    acc[lane, 0], acc[lane, 1] = real, imag
                    for part in range(2):
                        out[z, slot, :, pl.ds(part * BINS + lane * 128, 128)] = pair_sums(acc.at[lane, part])

        @pl.when(info[USED + slot] == 0)
        def _():
            for z in range(2):
                out[z, slot] = jnp.zeros((HALF, LENGTH), jnp.float32)


def dealt_products(width, info, own, one, two):
    return pl.pallas_call(
        lambda *refs: dealt_products_kernel(width, *refs),
        out_shape=jax.ShapeDtypeStruct((2, PCAP, HALF, LENGTH), jnp.float32),
        in_specs=[SMEM] + [ANY] * 3,
        out_specs=VMEM,
        scratch_shapes=[
            pltpu.VMEM((PCAP, 2, ROWS, LENGTH), jnp.bfloat16),
            pltpu.VMEM((BINS // 128, 2, 2 * HALF, 128), jnp.float32),
            pltpu.SemaphoreType.DMA((PCAP, 2)),
        ],
        compiler_params=PARAMS,
        cost_estimate=pl.CostEstimate(flops=1 << 25, bytes_accessed=8 << 20, transcendentals=0),
        name="dealt_products",
    )(info, own, one, two)


def path(records, info, deal, raw, width):
    far = lax.axis_index("win") // 8
    basis = jnp.asarray(basis_table())
    x = records.reshape(BLOCKS, 16, CHUNKS, HALF, 2, LENGTH)
    chip_groups = [[z * 8 + j for j in range(8)] for z in range(2)]
    far_groups = [[z * 8 + j for z in range(2)] for j in range(8)]

    dealt = lax.all_to_all(deal, "win", 0, 0, tiled=True, axis_index_groups=chip_groups)
    if raw is None:
        raw = raw_lanes(width, info, x)
    raw_one, raw_two = [lax.ppermute(lane, "chan", swap) for lane, swap in zip(raw, SWAPS)]
    sent = dealt_lanes(width, info, dealt, basis)
    raw_basis, *sent = lax.optimization_barrier((basis, *sent))
    came = [lax.ppermute(lane, "chan", swap) for lane, swap in zip(sent, SWAPS)]
    own = spectra(BLOCKS, lambda block: (block, slice(None), 0), x, basis)
    one = spectra(width, lambda spot: (spot,), raw_one, raw_basis)

    part = raw_products(width, info, raw_basis, own, one, raw_two)
    first = lax.all_to_all(part, "win", 0, 0, tiled=True, axis_index_groups=chip_groups)
    dealt, part = lax.optimization_barrier((dealt, part))
    second = dealt_products(width, info, dealt_spectra(dealt, basis), *came)
    first, second = lax.optimization_barrier((first, second))
    first = jnp.sum(first.astype(jnp.float32), axis=0).reshape(PCAP, 2, HALF, LENGTH)

    def half(at):
        return jnp.concatenate(
            [
                lax.dynamic_index_in_dim(first, at, axis=1, keepdims=False),
                lax.dynamic_index_in_dim(second, at, axis=0, keepdims=False),
            ],
            axis=1,
        )

    give = half(1 - far).astype(jnp.bfloat16)

    def swapped(slots):
        got = lax.all_gather(give[:slots], "win", axis=0, tiled=True, axis_index_groups=far_groups)
        got = lax.dynamic_slice_in_dim(got, (1 - far) * slots, slots, axis=0).astype(jnp.float32)
        return jnp.concatenate([got, jnp.zeros((PCAP - slots,) + got.shape[1:], jnp.float32)], axis=0)

    got = lax.cond(info[USED + 2] > 0, lambda: swapped(PCAP), lambda: swapped(PCAP // 2))
    return half(far) + got


def local(records, pairs, owner):
    where = lax.axis_index("chan")[None].astype(jnp.int32)
    x = records.reshape(BLOCKS, 16, CHUNKS, HALF, 2, LENGTH)
    narrow, wide, three, deal, *raw = prepare(where, pairs, owner, x)
    return lax.cond(
        three.reshape(()) == 0,
        lambda: path(records, narrow, deal, raw, 2),
        lambda: path(records, wide, deal, None, BLOCKS),
    )


def solution(mesh):
    return jax.shard_map(
        local,
        mesh=mesh,
        in_specs=(P("chan", None, "win", None), P(), P()),
        out_specs=P("chan", "win", None),
        check_vma=False,
    )
```

```python
import math

import jax
import jax.numpy as jnp
import ml_dtypes
import numpy as np
from jax import lax
from jax.experimental import pallas as pl
from jax.experimental.pallas import tpu as pltpu
from jax.sharding import PartitionSpec as P

PCAP = 4
BLOCKS = 3
CHAN = 32
CHUNKS = 2
LENGTH = 1024
BINS = 512
HALF = 16 // CHUNKS
ROWS = 512 // CHUNKS
VMEM = pl.BlockSpec(memory_space=pltpu.VMEM)
SMEM = pl.BlockSpec(memory_space=pltpu.SMEM)
ANY = pl.BlockSpec(memory_space=pl.ANY)
HBM = pl.BlockSpec(memory_space=pltpu.HBM)
PARAMS = pltpu.CompilerParams(vmem_limit_bytes=40 << 20)
ALL_VMEM = pltpu.CompilerParams(vmem_limit_bytes=63 << 20)


def basis_table():
    sample_ids = np.arange(LENGTH, dtype=np.int32)
    bin_ids = np.arange(BINS, dtype=np.int32)
    step = np.float32(2.0 * math.pi / LENGTH)
    phases = (sample_ids[:, None] * bin_ids[None, :] % LENGTH).astype(np.float32) * step
    taper = np.float32(0.5) - np.float32(0.5) * np.cos(sample_ids.astype(np.float32) * step)
    table = np.concatenate([taper[:, None] * np.cos(phases), -taper[:, None] * np.sin(phases)], axis=1)
    return table.astype(ml_dtypes.bfloat16)


LANES, FIRST, SECOND, USED, TABLE = 0, 6, 10, 14, 18
SWAPS = [
    [pair for low in range(start, CHAN - 1, 2) for pair in ((low, low + 1), (low + 1, low))] for start in (1, 0)
]


def fill_tables(where, pairs, owner, narrow, wide, flag, rows):
    odd = where[0] % 2
    me = where[0].astype(jnp.float32)
    count = owner.shape[1]
    rows[...] = jnp.full(rows.shape, -1000.0, jnp.float32)
    rows[0:2, 0:count] = pairs[...].astype(jnp.float32)
    rows[2:3, 0:count] = owner[...].astype(jnp.float32)
    first = rows[0:1, :]
    second = rows[1:2, :]
    holder = rows[2:3, :]

    chan = lax.broadcasted_iota(jnp.int32, (CHAN, 128), 0).astype(jnp.float32)

    def all_three(block, step):
        hits = [
            jnp.max(jnp.where((block == BLOCKS * chan + i) & (holder == chan + step), 1.0, 0.0), axis=1, keepdims=True)
            for i in range(BLOCKS)
        ]
        return hits[0] * hits[1] * hits[2]

    most = jnp.max(jnp.maximum(all_three(first, 1.0), all_three(second, -1.0)))

    def total(hit, value=1.0):
        return jnp.sum(jnp.where(hit, value, 0.0))

    first = first - BLOCKS * me
    second = second - BLOCKS * me
    apart = holder - me
    mine = apart == 0.0

    def needs(hit, block):
        return [(total(hit & (block == float(i))) > 0.0).astype(jnp.int32) for i in range(BLOCKS)]

    to_right = needs(apart == 1.0, first)
    to_left = needs(apart == -1.0, second)
    of_left = needs(mine, first + BLOCKS)
    of_right = needs(mine, second - BLOCKS)
    earlier = lax.broadcasted_iota(jnp.int32, (128, 128), 0) < lax.broadcasted_iota(jnp.int32, (128, 128), 1)
    ranks = jnp.dot(
        jnp.broadcast_to(jnp.where(mine, 1.0, 0.0), (8, 128)).astype(jnp.bfloat16),
        jnp.where(earlier, 1.0, 0.0).astype(jnp.bfloat16),
        preferred_element_type=jnp.float32,
    )[0:1, :]
    number = total(mine).astype(jnp.int32)

    def spot(need, block, width):
        if width == BLOCKS:
            return block
        return jnp.where(block == 0, 0, jnp.where(block == 1, need[0], jnp.minimum(need[0] + need[1], width - 1)))

    def picks(need, width):
        if width == BLOCKS:
            return [jnp.int32(i) for i in range(BLOCKS)]
        n0, n1, n2 = [n > 0 for n in need]
        lowest = jnp.where(n0, 0, jnp.where(n1, 1, jnp.where(n2, 2, 0)))
        after = jnp.where(n0 & n1, 1, jnp.where(n2 & (n0 | n1), 2, lowest))
        return [lowest.astype(jnp.int32), after.astype(jnp.int32), jnp.int32(0)]

    flag[0] = most.astype(jnp.int32)
    for info, width in ((narrow, 2), (wide, BLOCKS)):
        for i, (right, left) in enumerate(zip(picks(to_right, width), picks(to_left, width))):
            info[LANES + i] = jnp.where(odd == 1, right, left)
            info[LANES + 3 + i] = jnp.where(odd == 1, left, right)
    for slot in range(PCAP):
        hit = mine & (ranks == float(slot))
        a = total(hit, first).astype(jnp.int32)
        b = total(hit, second).astype(jnp.int32)
        used = (number > slot).astype(jnp.int32)
        for info, width in ((narrow, 2), (wide, BLOCKS)):
            from_left = BLOCKS + odd * width
            from_right = BLOCKS + (1 - odd) * width
            info[FIRST + slot] = jnp.where(a < 0, from_left + spot(of_left, a + BLOCKS, width), a)
            info[SECOND + slot] = jnp.where(b >= BLOCKS, from_right + spot(of_right, b - BLOCKS, width), b)
            info[USED + slot] = used


def whitened(rows, basis):
    spectrum = jnp.dot(rows, basis, preferred_element_type=jnp.float32)
    power_mean = jnp.mean(spectrum * spectrum, axis=-1, keepdims=True)
    return (spectrum * lax.rsqrt(power_mean + 1e-06)).astype(jnp.bfloat16)


COST = pl.CostEstimate(flops=2 * 3 * ROWS * LENGTH * LENGTH, bytes_accessed=8 << 20, transcendentals=0)


def lane_copy(buf, block, lanes, way, spot, lsem):
    return pltpu.make_async_copy(buf.at[block], lanes[way].at[spot], lsem.at[way, spot])


def start_lanes(width, info, buf, block, lanes, lsem):
    for way in range(2):
        for spot in range(width):

            @pl.when(info[LANES + way * 3 + spot] == block)
            def _(way=way, spot=spot):
                lane_copy(buf, block, lanes, way, spot, lsem).start()


def wait_lanes(width, buf, lanes, lsem):
    for way in range(2):
        for spot in range(width):
            lane_copy(buf, 0, lanes, way, spot, lsem).wait()


def raw_lanes_kernel(width, info, x, one, two, buf, xsem, lsem):
    loads = [pltpu.make_async_copy(x.at[block, :, 0], buf.at[block], xsem.at[block]) for block in range(BLOCKS)]
    for copy in loads:
        copy.start()
    for block, copy in enumerate(loads):
        copy.wait()
        start_lanes(width, info, buf, block, (one, two), lsem)
    wait_lanes(width, buf, (one, two), lsem)


def raw_lanes(width, info, x):
    lane = jax.ShapeDtypeStruct((width, 16, HALF, 2, LENGTH), jnp.bfloat16)
    return pl.pallas_call(
        lambda *refs: raw_lanes_kernel(width, *refs),
        out_shape=(lane, lane),
        in_specs=[SMEM, HBM],
        out_specs=[ANY] * 2,
        scratch_shapes=[
            pltpu.VMEM((BLOCKS, 16, HALF, 2, LENGTH), jnp.bfloat16),
            pltpu.SemaphoreType.DMA((BLOCKS,)),
            pltpu.SemaphoreType.DMA((2, width)),
        ],
        compiler_params=PARAMS,
        cost_estimate=pl.CostEstimate(flops=0, bytes_accessed=4 << 20, transcendentals=0),
        name="raw_lanes",
    )(info, x)


def prepare_kernel(where, pairs, owner, x, narrow, wide, flag, deal, one, two, *scratch):
    pairs_here, owner_here, rows, psem, buf, xsem, dsem, lsem = scratch
    small = [
        pltpu.make_async_copy(pairs, pairs_here, psem.at[0]),
        pltpu.make_async_copy(owner, owner_here, psem.at[1]),
    ]
    for copy in small:
        copy.start()
    loads = [
        [pltpu.make_async_copy(x.at[block, :, chunk], buf.at[chunk, block], xsem.at[chunk, block]) for block in range(BLOCKS)]
        for chunk in range(CHUNKS)
    ]
    for copies in reversed(loads):
        for copy in copies:
            copy.start()
    deals = [
        [
            pltpu.make_async_copy(buf.at[1, block, pl.ds(z * 8, 8)], deal.at[:, block, z], dsem.at[block, z])
            for z in range(2)
        ]
        for block in range(BLOCKS)
    ]
    for block in range(BLOCKS):
        loads[1][block].wait()
        for copy in deals[block]:
            copy.start()
    for copy in small:
        copy.wait()
    fill_tables(where, pairs_here, owner_here, narrow, wide, flag, rows)
    for block in range(BLOCKS):
        loads[0][block].wait()
        start_lanes(2, narrow, buf.at[0], block, (one, two), lsem)
    for copies in deals:
        for copy in copies:
            copy.wait()
    wait_lanes(2, buf.at[0], (one, two), lsem)


def prepare(where, pairs, owner, x):
    table = jax.ShapeDtypeStruct((TABLE,), jnp.int32)
    lane = jax.ShapeDtypeStruct((2, 16, HALF, 2, LENGTH), jnp.bfloat16)
    return pl.pallas_call(
        prepare_kernel,
        out_shape=(
            table,
            table,
            jax.ShapeDtypeStruct((1,), jnp.int32),
            jax.ShapeDtypeStruct((8, BLOCKS, 2, HALF, 2, LENGTH), jnp.bfloat16),
            lane,
            lane,
        ),
        in_specs=[SMEM, HBM, HBM, HBM],
        out_specs=[SMEM] * 3 + [ANY] * 3,
        scratch_shapes=[
            pltpu.VMEM((2, pairs.shape[0]), jnp.int32),
            pltpu.VMEM((1, pairs.shape[0]), jnp.int32),
            pltpu.VMEM((8, 128), jnp.float32),
            pltpu.SemaphoreType.DMA((2,)),
            pltpu.VMEM((CHUNKS, BLOCKS, 16, HALF, 2, LENGTH), jnp.bfloat16),
            pltpu.SemaphoreType.DMA((CHUNKS, BLOCKS)),
            pltpu.SemaphoreType.DMA((BLOCKS, 2)),
            pltpu.SemaphoreType.DMA((2, 2)),
        ],
        compiler_params=ALL_VMEM,
        cost_estimate=pl.CostEstimate(flops=0, bytes_accessed=7 << 20, transcendentals=0),
        name="prepare",
    )(where, pairs.T, owner[None], x)


def taken(info, spot):
    hits = [
        (info[USED + slot] > 0) & ((info[FIRST + slot] == spot) | (info[SECOND + slot] == spot)) for slot in range(PCAP)
    ]
    return hits[0] | hits[1] | hits[2] | hits[3]


def spectra_kernel(count, base, at, info, x, basis, own, xbuf, spec, xsem, osem):
    def load(block):
        return pltpu.make_async_copy(x.at[at(block)], xbuf.at[block], xsem.at[block])

    def store(block):
        return pltpu.make_async_copy(spec.at[block], own.at[block], osem.at[block])

    for block in range(count):
        load(block).start()
    for block in range(count):
        load(block).wait()

        @pl.when(taken(info, base + block))
        def _(block=block):
            spec[block] = whitened(xbuf[block].reshape(ROWS, LENGTH), basis[...])

        store(block).start()
    for block in range(count):
        store(block).wait()


def spectra(count, base, at, info, x, basis):
    return pl.pallas_call(
        lambda *refs: spectra_kernel(count, base, at, *refs),
        out_shape=jax.ShapeDtypeStruct((count, ROWS, LENGTH), jnp.bfloat16),
        in_specs=[SMEM, HBM, VMEM],
        out_specs=ANY,
        scratch_shapes=[
            pltpu.VMEM((count, 16, HALF, 2, LENGTH), jnp.bfloat16),
            pltpu.VMEM((count, ROWS, LENGTH), jnp.bfloat16),
            pltpu.SemaphoreType.DMA((count,)),
            pltpu.SemaphoreType.DMA((count,)),
        ],
        compiler_params=PARAMS,
        cost_estimate=COST,
        name="spectra",
    )(info, x, basis)


def dealt_kernel(width, info, x, basis, one, two, spec, lsem):
    for block in range(BLOCKS):
        picks = [info[LANES + way * 3 + spot] == block for way in range(2) for spot in range(width)]
        wanted = picks[0]
        for pick in picks[1:]:
            wanted = wanted | pick

        @pl.when(wanted)
        def _(block=block):
            spec[block] = whitened(x[:, block].reshape(ROWS, LENGTH), basis[...])
            start_lanes(width, info, spec, block, (one, two), lsem)

    wait_lanes(width, spec, (one, two), lsem)


def dealt_lanes(width, info, x, basis):
    lane = jax.ShapeDtypeStruct((width, ROWS, LENGTH), jnp.bfloat16)
    return pl.pallas_call(
        lambda *refs: dealt_kernel(width, *refs),
        out_shape=(lane, lane),
        in_specs=[SMEM, VMEM, VMEM],
        out_specs=[HBM] * 2,
        scratch_shapes=[
            pltpu.VMEM((BLOCKS, ROWS, LENGTH), jnp.bfloat16),
            pltpu.SemaphoreType.DMA((2, width)),
        ],
        compiler_params=PARAMS,
        cost_estimate=COST,
        name="dealt_lanes",
    )(info, x, basis)


def dealt_own_kernel(x, basis, own):
    for block in range(BLOCKS):
        own[block] = whitened(x[:, block].reshape(ROWS, LENGTH), basis[...])


def dealt_spectra(x, basis):
    return pl.pallas_call(
        dealt_own_kernel,
        out_shape=jax.ShapeDtypeStruct((BLOCKS, ROWS, LENGTH), jnp.bfloat16),
        in_specs=[VMEM, VMEM],
        out_specs=VMEM,
        compiler_params=PARAMS,
        cost_estimate=COST,
        name="dealt_spectra",
    )(x, basis)


def parts(read, at, lane):
    a_re, a_im, b_re, b_im = [
        read(operand, at, pl.ds(start + lane * 128, 128)).astype(jnp.float32)
        for operand in range(2)
        for start in (0, BINS)
    ]
    return a_re * b_re + a_im * b_im, a_im * b_re - a_re * b_im


def pair_sums(acc):
    return acc[pl.ds(0, HALF, 2), :] + acc[pl.ds(1, HALF, 2), :]


def tile(index):
    return pl.ds(pl.multiple_of(index * 2 * HALF, 2 * HALF), 2 * HALF)


def raw_products_kernel(width, info, basis, own, one, two, out, xbuf, buf, acc, xsem, osem):
    loads = [pltpu.make_async_copy(two.at[spot], xbuf.at[spot], xsem.at[spot]) for spot in range(width)]
    ready = [
        pltpu.make_async_copy(own, buf.at[pl.ds(0, BLOCKS)], osem.at[0]),
        pltpu.make_async_copy(one, buf.at[pl.ds(BLOCKS, width)], osem.at[1]),
    ]
    for copy in loads + ready:
        copy.start()
    for spot, copy in enumerate(loads):
        copy.wait()

        @pl.when(taken(info, BLOCKS + width + spot))
        def _(spot=spot):
            buf[BLOCKS + width + spot] = whitened(xbuf[spot].reshape(ROWS, LENGTH), basis[...])

    for copy in ready:
        copy.wait()

    @pl.loop(0, PCAP)
    def _(slot):
        spots = info[FIRST + slot], info[SECOND + slot]

        def read(operand, at, part):
            return buf[spots[operand], at, part]

        @pl.when(info[USED + slot] > 0)
        def _():
            @pl.loop(0, 8)
            def _(peer):
                for lane in range(BINS // 128):
                    for z in range(2):
                        acc[lane, z, 0], acc[lane, z, 1] = parts(read, tile(z * 8 + peer), lane)
                    for part in range(2):
                        sums = [pair_sums(acc.at[lane, z, part]) for z in range(2)]
                        out[peer, slot, :, pl.ds(part * BINS + lane * 128, 128)] = jnp.concatenate(
                            sums, axis=0
                        ).astype(jnp.bfloat16)

        @pl.when(info[USED + slot] == 0)
        def _():
            @pl.loop(0, 8)
            def _(peer):
                out[peer, slot] = jnp.zeros((2 * HALF, LENGTH), jnp.bfloat16)


def raw_products(width, info, basis, own, one, two):
    return pl.pallas_call(
        lambda *refs: raw_products_kernel(width, *refs),
        out_shape=jax.ShapeDtypeStruct((8, PCAP, 2 * HALF, LENGTH), jnp.bfloat16),
        in_specs=[SMEM, VMEM, ANY, ANY, HBM],
        out_specs=VMEM,
        scratch_shapes=[
            pltpu.VMEM((width, 16, HALF, 2, LENGTH), jnp.bfloat16),
            pltpu.VMEM((BLOCKS + 2 * width, ROWS, LENGTH), jnp.bfloat16),
            pltpu.VMEM((BINS // 128, 2, 2, 2 * HALF, 128), jnp.float32),
            pltpu.SemaphoreType.DMA((width,)),
            pltpu.SemaphoreType.DMA((2,)),
        ],
        compiler_params=PARAMS,
        cost_estimate=COST,
        name="raw_products",
    )(info, basis, own, one, two)


def dealt_products_kernel(width, info, own, one, two, out, buf, acc, sems):
    def start(slot, operand, spot):
        to, sem = buf.at[slot, operand], sems.at[slot, operand]

        @pl.when(spot < BLOCKS)
        def _():
            pltpu.make_async_copy(own.at[spot], to, sem).start()

        @pl.when((spot >= BLOCKS) & (spot < BLOCKS + width))
        def _():
            pltpu.make_async_copy(one.at[spot - BLOCKS], to, sem).start()

        @pl.when(spot >= BLOCKS + width)
        def _():
            pltpu.make_async_copy(two.at[spot - BLOCKS - width], to, sem).start()

    for slot in range(PCAP):

        @pl.when(info[USED + slot] > 0)
        def _(slot=slot):
            start(slot, 0, info[FIRST + slot])
            start(slot, 1, info[SECOND + slot])

    @pl.loop(0, PCAP)
    def _(slot):
        def read(operand, at, part):
            return buf[slot, operand, at, part]

        @pl.when(info[USED + slot] > 0)
        def _():
            for operand in range(2):
                pltpu.make_async_copy(own.at[0], buf.at[slot, operand], sems.at[slot, operand]).wait()

            @pl.loop(0, 2)
            def _(z):
                for lane in range(BINS // 128):
                    real, imag = parts(read, tile(z), lane)
                    for source in range(1, 8):
                        re, im = parts(read, tile(source * 2 + z), lane)
                        real, imag = real + re, imag + im
                    acc[lane, 0], acc[lane, 1] = real, imag
                    for part in range(2):
                        out[z, slot, :, pl.ds(part * BINS + lane * 128, 128)] = pair_sums(acc.at[lane, part])

        @pl.when(info[USED + slot] == 0)
        def _():
            for z in range(2):
                out[z, slot] = jnp.zeros((HALF, LENGTH), jnp.float32)


def dealt_products(width, info, own, one, two):
    return pl.pallas_call(
        lambda *refs: dealt_products_kernel(width, *refs),
        out_shape=jax.ShapeDtypeStruct((2, PCAP, HALF, LENGTH), jnp.float32),
        in_specs=[SMEM] + [ANY] * 3,
        out_specs=VMEM,
        scratch_shapes=[
            pltpu.VMEM((PCAP, 2, ROWS, LENGTH), jnp.bfloat16),
            pltpu.VMEM((BINS // 128, 2, 2 * HALF, 128), jnp.float32),
            pltpu.SemaphoreType.DMA((PCAP, 2)),
        ],
        compiler_params=PARAMS,
        cost_estimate=pl.CostEstimate(flops=1 << 25, bytes_accessed=8 << 20, transcendentals=0),
        name="dealt_products",
    )(info, own, one, two)


def path(records, info, deal, raw, width):
    far = lax.axis_index("win") // 8
    basis = jnp.asarray(basis_table())
    x = records.reshape(BLOCKS, 16, CHUNKS, HALF, 2, LENGTH)
    chip_groups = [[z * 8 + j for j in range(8)] for z in range(2)]
    far_groups = [[z * 8 + j for z in range(2)] for j in range(8)]

    dealt = lax.all_to_all(deal, "win", 0, 0, tiled=True, axis_index_groups=chip_groups)
    if raw is None:
        raw = raw_lanes(width, info, x)
    raw_one, raw_two = [lax.ppermute(lane, "chan", swap) for lane, swap in zip(raw, SWAPS)]
    sent = dealt_lanes(width, info, dealt, basis)
    raw_basis, *sent = lax.optimization_barrier((basis, *sent))
    came = [lax.ppermute(lane, "chan", swap) for lane, swap in zip(sent, SWAPS)]
    own = spectra(BLOCKS, 0, lambda block: (block, slice(None), 0), info, x, basis)
    one = spectra(width, BLOCKS, lambda spot: (spot,), info, raw_one, raw_basis)

    part = raw_products(width, info, raw_basis, own, one, raw_two)
    first = lax.all_to_all(part, "win", 0, 0, tiled=True, axis_index_groups=chip_groups)
    dealt, part = lax.optimization_barrier((dealt, part))
    second = dealt_products(width, info, dealt_spectra(dealt, basis), *came)
    first, second = lax.optimization_barrier((first, second))
    first = jnp.sum(first.astype(jnp.float32), axis=0).reshape(PCAP, 2, HALF, LENGTH)

    def half(at):
        return jnp.concatenate(
            [
                lax.dynamic_index_in_dim(first, at, axis=1, keepdims=False),
                lax.dynamic_index_in_dim(second, at, axis=0, keepdims=False),
            ],
            axis=1,
        )

    give = half(1 - far).astype(jnp.bfloat16)

    def swapped(slots):
        got = lax.all_gather(give[:slots], "win", axis=0, tiled=True, axis_index_groups=far_groups)
        got = lax.dynamic_slice_in_dim(got, (1 - far) * slots, slots, axis=0).astype(jnp.float32)
        return jnp.concatenate([got, jnp.zeros((PCAP - slots,) + got.shape[1:], jnp.float32)], axis=0)

    got = lax.cond(info[USED + 2] > 0, lambda: swapped(PCAP), lambda: swapped(PCAP // 2))
    return half(far) + got


def local(records, pairs, owner):
    where = lax.axis_index("chan")[None].astype(jnp.int32)
    x = records.reshape(BLOCKS, 16, CHUNKS, HALF, 2, LENGTH)
    narrow, wide, three, deal, *raw = prepare(where, pairs, owner, x)
    return lax.cond(
        three.reshape(()) == 0,
        lambda: path(records, narrow, deal, raw, 2),
        lambda: path(records, wide, deal, None, BLOCKS),
    )


def solution(mesh):
    return jax.shard_map(
        local,
        mesh=mesh,
        in_specs=(P("chan", None, "win", None), P(), P()),
        out_specs=P("chan", "win", None),
        check_vma=False,
    )
```

```python
import math

import jax
import jax.numpy as jnp
import ml_dtypes
import numpy as np
from jax import lax
from jax.experimental import pallas as pl
from jax.experimental.pallas import tpu as pltpu
from jax.sharding import PartitionSpec as P

PCAP = 4
BLOCKS = 3
CHAN = 32
CHUNKS = 2
LENGTH = 1024
BINS = 512
HALF = 16 // CHUNKS
ROWS = 512 // CHUNKS
VMEM = pl.BlockSpec(memory_space=pltpu.VMEM)
SMEM = pl.BlockSpec(memory_space=pltpu.SMEM)
ANY = pl.BlockSpec(memory_space=pl.ANY)
HBM = pl.BlockSpec(memory_space=pltpu.HBM)
PARAMS = pltpu.CompilerParams(vmem_limit_bytes=40 << 20)
ALL_VMEM = pltpu.CompilerParams(vmem_limit_bytes=63 << 20)


def basis_table():
    sample_ids = np.arange(LENGTH, dtype=np.int32)
    bin_ids = np.arange(BINS, dtype=np.int32)
    step = np.float32(2.0 * math.pi / LENGTH)
    phases = (sample_ids[:, None] * bin_ids[None, :] % LENGTH).astype(np.float32) * step
    taper = np.float32(0.5) - np.float32(0.5) * np.cos(sample_ids.astype(np.float32) * step)
    table = np.concatenate([taper[:, None] * np.cos(phases), -taper[:, None] * np.sin(phases)], axis=1)
    return table.astype(ml_dtypes.bfloat16)


LANES, FIRST, SECOND, USED, TABLE = 0, 6, 10, 14, 18
SWAPS = [
    [pair for low in range(start, CHAN - 1, 2) for pair in ((low, low + 1), (low + 1, low))] for start in (1, 0)
]


def fill_tables(where, pairs, owner, narrow, wide, flag, rows):
    odd = where[0] % 2
    me = where[0].astype(jnp.float32)
    count = owner.shape[1]
    rows[...] = jnp.full(rows.shape, -1000.0, jnp.float32)
    rows[0:2, 0:count] = pairs[...].astype(jnp.float32)
    rows[2:3, 0:count] = owner[...].astype(jnp.float32)
    first = rows[0:1, :]
    second = rows[1:2, :]
    holder = rows[2:3, :]

    chan = lax.broadcasted_iota(jnp.int32, (CHAN, 128), 0).astype(jnp.float32)

    def all_three(block, step):
        hits = [
            jnp.max(jnp.where((block == BLOCKS * chan + i) & (holder == chan + step), 1.0, 0.0), axis=1, keepdims=True)
            for i in range(BLOCKS)
        ]
        return hits[0] * hits[1] * hits[2]

    most = jnp.max(jnp.maximum(all_three(first, 1.0), all_three(second, -1.0)))

    def total(hit, value=1.0):
        return jnp.sum(jnp.where(hit, value, 0.0))

    first = first - BLOCKS * me
    second = second - BLOCKS * me
    apart = holder - me
    mine = apart == 0.0

    def needs(hit, block):
        return [(total(hit & (block == float(i))) > 0.0).astype(jnp.int32) for i in range(BLOCKS)]

    to_right = needs(apart == 1.0, first)
    to_left = needs(apart == -1.0, second)
    of_left = needs(mine, first + BLOCKS)
    of_right = needs(mine, second - BLOCKS)
    earlier = lax.broadcasted_iota(jnp.int32, (128, 128), 0) < lax.broadcasted_iota(jnp.int32, (128, 128), 1)
    ranks = jnp.dot(
        jnp.broadcast_to(jnp.where(mine, 1.0, 0.0), (8, 128)).astype(jnp.bfloat16),
        jnp.where(earlier, 1.0, 0.0).astype(jnp.bfloat16),
        preferred_element_type=jnp.float32,
    )[0:1, :]
    number = total(mine).astype(jnp.int32)

    def spot(need, block, width):
        if width == BLOCKS:
            return block
        return jnp.where(block == 0, 0, jnp.where(block == 1, need[0], jnp.minimum(need[0] + need[1], width - 1)))

    def picks(need, width):
        if width == BLOCKS:
            return [jnp.int32(i) for i in range(BLOCKS)]
        n0, n1, n2 = [n > 0 for n in need]
        lowest = jnp.where(n0, 0, jnp.where(n1, 1, jnp.where(n2, 2, 0)))
        after = jnp.where(n0 & n1, 1, jnp.where(n2 & (n0 | n1), 2, lowest))
        return [lowest.astype(jnp.int32), after.astype(jnp.int32), jnp.int32(0)]

    flag[0] = most.astype(jnp.int32)
    for info, width in ((narrow, 2), (wide, BLOCKS)):
        for i, (right, left) in enumerate(zip(picks(to_right, width), picks(to_left, width))):
            info[LANES + i] = jnp.where(odd == 1, right, left)
            info[LANES + 3 + i] = jnp.where(odd == 1, left, right)
    for slot in range(PCAP):
        hit = mine & (ranks == float(slot))
        a = total(hit, first).astype(jnp.int32)
        b = total(hit, second).astype(jnp.int32)
        used = (number > slot).astype(jnp.int32)
        for info, width in ((narrow, 2), (wide, BLOCKS)):
            from_left = BLOCKS + odd * width
            from_right = BLOCKS + (1 - odd) * width
            info[FIRST + slot] = jnp.where(a < 0, from_left + spot(of_left, a + BLOCKS, width), a)
            info[SECOND + slot] = jnp.where(b >= BLOCKS, from_right + spot(of_right, b - BLOCKS, width), b)
            info[USED + slot] = used


def whitened(rows, basis):
    spectrum = jnp.dot(rows, basis, preferred_element_type=jnp.float32)
    power_mean = jnp.mean(spectrum * spectrum, axis=-1, keepdims=True)
    return (spectrum * lax.rsqrt(power_mean + 1e-06)).astype(jnp.bfloat16)


COST = pl.CostEstimate(flops=2 * 3 * ROWS * LENGTH * LENGTH, bytes_accessed=8 << 20, transcendentals=0)


def lane_copy(buf, block, lanes, way, spot, lsem):
    return pltpu.make_async_copy(buf.at[block], lanes[way].at[spot], lsem.at[way, spot])


def start_lanes(width, info, buf, block, lanes, lsem):
    for way in range(2):
        for spot in range(width):

            @pl.when(info[LANES + way * 3 + spot] == block)
            def _(way=way, spot=spot):
                lane_copy(buf, block, lanes, way, spot, lsem).start()


def wait_lanes(width, buf, lanes, lsem):
    for way in range(2):
        for spot in range(width):
            lane_copy(buf, 0, lanes, way, spot, lsem).wait()


def raw_lanes_kernel(width, info, x, one, two, buf, xsem, lsem):
    loads = [pltpu.make_async_copy(x.at[block, :, 0], buf.at[block], xsem.at[block]) for block in range(BLOCKS)]
    for copy in loads:
        copy.start()
    for block, copy in enumerate(loads):
        copy.wait()
        start_lanes(width, info, buf, block, (one, two), lsem)
    wait_lanes(width, buf, (one, two), lsem)


def raw_lanes(width, info, x):
    lane = jax.ShapeDtypeStruct((width, 16, HALF, 2, LENGTH), jnp.bfloat16)
    return pl.pallas_call(
        lambda *refs: raw_lanes_kernel(width, *refs),
        out_shape=(lane, lane),
        in_specs=[SMEM, HBM],
        out_specs=[ANY] * 2,
        scratch_shapes=[
            pltpu.VMEM((BLOCKS, 16, HALF, 2, LENGTH), jnp.bfloat16),
            pltpu.SemaphoreType.DMA((BLOCKS,)),
            pltpu.SemaphoreType.DMA((2, width)),
        ],
        compiler_params=PARAMS,
        cost_estimate=pl.CostEstimate(flops=0, bytes_accessed=4 << 20, transcendentals=0),
        name="raw_lanes",
    )(info, x)


def prepare_kernel(where, pairs, owner, x, narrow, wide, flag, deal, one, two, *scratch):
    pairs_here, owner_here, rows, psem, buf, xsem, dsem, lsem = scratch
    small = [
        pltpu.make_async_copy(pairs, pairs_here, psem.at[0]),
        pltpu.make_async_copy(owner, owner_here, psem.at[1]),
    ]
    for copy in small:
        copy.start()
    loads = [
        [pltpu.make_async_copy(x.at[block, :, chunk], buf.at[chunk, block], xsem.at[chunk, block]) for block in range(BLOCKS)]
        for chunk in range(CHUNKS)
    ]
    for copies in reversed(loads):
        for copy in copies:
            copy.start()
    deals = [
        [
            pltpu.make_async_copy(buf.at[1, block, pl.ds(z * 8, 8)], deal.at[:, block, z], dsem.at[block, z])
            for z in range(2)
        ]
        for block in range(BLOCKS)
    ]
    for block in range(BLOCKS):
        loads[1][block].wait()
        for copy in deals[block]:
            copy.start()
    for copy in small:
        copy.wait()
    fill_tables(where, pairs_here, owner_here, narrow, wide, flag, rows)
    for block in range(BLOCKS):
        loads[0][block].wait()
        start_lanes(2, narrow, buf.at[0], block, (one, two), lsem)
    for copies in deals:
        for copy in copies:
            copy.wait()
    wait_lanes(2, buf.at[0], (one, two), lsem)


def prepare(where, pairs, owner, x):
    table = jax.ShapeDtypeStruct((TABLE,), jnp.int32)
    lane = jax.ShapeDtypeStruct((2, 16, HALF, 2, LENGTH), jnp.bfloat16)
    return pl.pallas_call(
        prepare_kernel,
        out_shape=(
            table,
            table,
            jax.ShapeDtypeStruct((1,), jnp.int32),
            jax.ShapeDtypeStruct((8, BLOCKS, 2, HALF, 2, LENGTH), jnp.bfloat16),
            lane,
            lane,
        ),
        in_specs=[SMEM, HBM, HBM, HBM],
        out_specs=[SMEM] * 3 + [ANY] * 3,
        scratch_shapes=[
            pltpu.VMEM((2, pairs.shape[0]), jnp.int32),
            pltpu.VMEM((1, pairs.shape[0]), jnp.int32),
            pltpu.VMEM((8, 128), jnp.float32),
            pltpu.SemaphoreType.DMA((2,)),
            pltpu.VMEM((CHUNKS, BLOCKS, 16, HALF, 2, LENGTH), jnp.bfloat16),
            pltpu.SemaphoreType.DMA((CHUNKS, BLOCKS)),
            pltpu.SemaphoreType.DMA((BLOCKS, 2)),
            pltpu.SemaphoreType.DMA((2, 2)),
        ],
        compiler_params=ALL_VMEM,
        cost_estimate=pl.CostEstimate(flops=0, bytes_accessed=7 << 20, transcendentals=0),
        name="prepare",
    )(where, pairs.T, owner[None], x)


def taken(info, spot):
    hits = [
        (info[USED + slot] > 0) & ((info[FIRST + slot] == spot) | (info[SECOND + slot] == spot)) for slot in range(PCAP)
    ]
    return hits[0] | hits[1] | hits[2] | hits[3]


def spectra_kernel(count, base, at, info, x, basis, own, xbuf, spec, xsem, osem):
    def load(block):
        return pltpu.make_async_copy(x.at[at(block)], xbuf.at[block], xsem.at[block])

    def store(block):
        return pltpu.make_async_copy(spec.at[block], own.at[block], osem.at[block])

    for block in range(count):
        load(block).start()
    for block in range(count):
        load(block).wait()

        @pl.when(taken(info, base + block))
        def _(block=block):
            spec[block] = whitened(xbuf[block].reshape(ROWS, LENGTH), basis[...])

        store(block).start()
    for block in range(count):
        store(block).wait()


def spectra(count, base, at, info, x, basis):
    return pl.pallas_call(
        lambda *refs: spectra_kernel(count, base, at, *refs),
        out_shape=jax.ShapeDtypeStruct((count, ROWS, LENGTH), jnp.bfloat16),
        in_specs=[SMEM, HBM, VMEM],
        out_specs=ANY,
        scratch_shapes=[
            pltpu.VMEM((count, 16, HALF, 2, LENGTH), jnp.bfloat16),
            pltpu.VMEM((count, ROWS, LENGTH), jnp.bfloat16),
            pltpu.SemaphoreType.DMA((count,)),
            pltpu.SemaphoreType.DMA((count,)),
        ],
        compiler_params=PARAMS,
        cost_estimate=COST,
        name="spectra",
    )(info, x, basis)


def dealt_kernel(width, info, x, basis, one, two, spec, lsem):
    for block in range(BLOCKS):
        picks = [info[LANES + way * 3 + spot] == block for way in range(2) for spot in range(width)]
        wanted = picks[0]
        for pick in picks[1:]:
            wanted = wanted | pick

        @pl.when(wanted)
        def _(block=block):
            spec[block] = whitened(x[:, block].reshape(ROWS, LENGTH), basis[...])
            start_lanes(width, info, spec, block, (one, two), lsem)

    wait_lanes(width, spec, (one, two), lsem)


def dealt_lanes(width, info, x, basis):
    lane = jax.ShapeDtypeStruct((width, ROWS, LENGTH), jnp.bfloat16)
    return pl.pallas_call(
        lambda *refs: dealt_kernel(width, *refs),
        out_shape=(lane, lane),
        in_specs=[SMEM, VMEM, VMEM],
        out_specs=[HBM] * 2,
        scratch_shapes=[
            pltpu.VMEM((BLOCKS, ROWS, LENGTH), jnp.bfloat16),
            pltpu.SemaphoreType.DMA((2, width)),
        ],
        compiler_params=PARAMS,
        cost_estimate=COST,
        name="dealt_lanes",
    )(info, x, basis)


def dealt_own_kernel(x, basis, own):
    for block in range(BLOCKS):
        own[block] = whitened(x[:, block].reshape(ROWS, LENGTH), basis[...])


def dealt_spectra(x, basis):
    return pl.pallas_call(
        dealt_own_kernel,
        out_shape=jax.ShapeDtypeStruct((BLOCKS, ROWS, LENGTH), jnp.bfloat16),
        in_specs=[VMEM, VMEM],
        out_specs=VMEM,
        compiler_params=PARAMS,
        cost_estimate=COST,
        name="dealt_spectra",
    )(x, basis)


def parts(read, at, lane):
    a_re, a_im, b_re, b_im = [
        read(operand, at, pl.ds(start + lane * 128, 128)).astype(jnp.float32)
        for operand in range(2)
        for start in (0, BINS)
    ]
    return a_re * b_re + a_im * b_im, a_im * b_re - a_re * b_im


def pair_sums(acc):
    return acc[pl.ds(0, HALF, 2), :] + acc[pl.ds(1, HALF, 2), :]


def tile(index):
    return pl.ds(pl.multiple_of(index * 2 * HALF, 2 * HALF), 2 * HALF)


def raw_products_kernel(width, info, basis, own, one, two, out, xbuf, buf, acc, xsem, osem):
    loads = [pltpu.make_async_copy(two.at[spot], xbuf.at[spot], xsem.at[spot]) for spot in range(width)]
    ready = [
        pltpu.make_async_copy(own, buf.at[pl.ds(0, BLOCKS)], osem.at[0]),
        pltpu.make_async_copy(one, buf.at[pl.ds(BLOCKS, width)], osem.at[1]),
    ]
    for copy in loads + ready:
        copy.start()
    for spot, copy in enumerate(loads):
        copy.wait()

        @pl.when(taken(info, BLOCKS + width + spot))
        def _(spot=spot):
            buf[BLOCKS + width + spot] = whitened(xbuf[spot].reshape(ROWS, LENGTH), basis[...])

    for copy in ready:
        copy.wait()

    @pl.loop(0, PCAP)
    def _(slot):
        spots = info[FIRST + slot], info[SECOND + slot]

        def read(operand, at, part):
            return buf[spots[operand], at, part]

        @pl.when(info[USED + slot] > 0)
        def _():
            @pl.loop(0, 8)
            def _(peer):
                for lane in range(BINS // 128):
                    for z in range(2):
                        acc[lane, z, 0], acc[lane, z, 1] = parts(read, tile(z * 8 + (peer + 4) % 8), lane)
                    for part in range(2):
                        sums = [pair_sums(acc.at[lane, z, part]) for z in range(2)]
                        out[peer, slot, :, pl.ds(part * BINS + lane * 128, 128)] = jnp.concatenate(
                            sums, axis=0
                        ).astype(jnp.bfloat16)

        @pl.when(info[USED + slot] == 0)
        def _():
            @pl.loop(0, 8)
            def _(peer):
                out[peer, slot] = jnp.zeros((2 * HALF, LENGTH), jnp.bfloat16)


def raw_products(width, info, basis, own, one, two):
    return pl.pallas_call(
        lambda *refs: raw_products_kernel(width, *refs),
        out_shape=jax.ShapeDtypeStruct((8, PCAP, 2 * HALF, LENGTH), jnp.bfloat16),
        in_specs=[SMEM, VMEM, ANY, ANY, HBM],
        out_specs=VMEM,
        scratch_shapes=[
            pltpu.VMEM((width, 16, HALF, 2, LENGTH), jnp.bfloat16),
            pltpu.VMEM((BLOCKS + 2 * width, ROWS, LENGTH), jnp.bfloat16),
            pltpu.VMEM((BINS // 128, 2, 2, 2 * HALF, 128), jnp.float32),
            pltpu.SemaphoreType.DMA((width,)),
            pltpu.SemaphoreType.DMA((2,)),
        ],
        compiler_params=PARAMS,
        cost_estimate=COST,
        name="raw_products",
    )(info, basis, own, one, two)


def dealt_products_kernel(width, info, own, one, two, out, buf, acc, sems):
    def start(slot, operand, spot):
        to, sem = buf.at[slot, operand], sems.at[slot, operand]

        @pl.when(spot < BLOCKS)
        def _():
            pltpu.make_async_copy(own.at[spot], to, sem).start()

        @pl.when((spot >= BLOCKS) & (spot < BLOCKS + width))
        def _():
            pltpu.make_async_copy(one.at[spot - BLOCKS], to, sem).start()

        @pl.when(spot >= BLOCKS + width)
        def _():
            pltpu.make_async_copy(two.at[spot - BLOCKS - width], to, sem).start()

    for slot in range(PCAP):

        @pl.when(info[USED + slot] > 0)
        def _(slot=slot):
            start(slot, 0, info[FIRST + slot])
            start(slot, 1, info[SECOND + slot])

    @pl.loop(0, PCAP)
    def _(slot):
        def read(operand, at, part):
            return buf[slot, operand, at, part]

        @pl.when(info[USED + slot] > 0)
        def _():
            for operand in range(2):
                pltpu.make_async_copy(own.at[0], buf.at[slot, operand], sems.at[slot, operand]).wait()

            @pl.loop(0, 2)
            def _(z):
                for lane in range(BINS // 128):
                    real, imag = parts(read, tile(z), lane)
                    for source in range(1, 8):
                        re, im = parts(read, tile(source * 2 + z), lane)
                        real, imag = real + re, imag + im
                    acc[lane, 0], acc[lane, 1] = real, imag
                    for part in range(2):
                        out[z, slot, :, pl.ds(part * BINS + lane * 128, 128)] = pair_sums(acc.at[lane, part])

        @pl.when(info[USED + slot] == 0)
        def _():
            for z in range(2):
                out[z, slot] = jnp.zeros((HALF, LENGTH), jnp.float32)


def dealt_products(width, info, own, one, two):
    return pl.pallas_call(
        lambda *refs: dealt_products_kernel(width, *refs),
        out_shape=jax.ShapeDtypeStruct((2, PCAP, HALF, LENGTH), jnp.float32),
        in_specs=[SMEM] + [ANY] * 3,
        out_specs=VMEM,
        scratch_shapes=[
            pltpu.VMEM((PCAP, 2, ROWS, LENGTH), jnp.bfloat16),
            pltpu.VMEM((BINS // 128, 2, 2 * HALF, 128), jnp.float32),
            pltpu.SemaphoreType.DMA((PCAP, 2)),
        ],
        compiler_params=PARAMS,
        cost_estimate=pl.CostEstimate(flops=1 << 25, bytes_accessed=8 << 20, transcendentals=0),
        name="dealt_products",
    )(info, own, one, two)


def path(records, info, deal, raw, width):
    far = lax.axis_index("win") // 8
    basis = jnp.asarray(basis_table())
    x = records.reshape(BLOCKS, 16, CHUNKS, HALF, 2, LENGTH)
    chip_groups = [[z * 8 + j for j in range(8)] for z in range(2)]
    turned_groups = [[z * 8 + (j + 4) % 8 for j in range(8)] for z in range(2)]
    far_groups = [[z * 8 + j for z in range(2)] for j in range(8)]

    dealt = lax.all_to_all(deal, "win", 0, 0, tiled=True, axis_index_groups=chip_groups)
    if raw is None:
        raw = raw_lanes(width, info, x)
    raw_one, raw_two = [lax.ppermute(lane, "chan", swap) for lane, swap in zip(raw, SWAPS)]
    sent = dealt_lanes(width, info, dealt, basis)
    raw_basis, *sent = lax.optimization_barrier((basis, *sent))
    came = [lax.ppermute(lane, "chan", swap) for lane, swap in zip(sent, SWAPS)]
    own = spectra(BLOCKS, 0, lambda block: (block, slice(None), 0), info, x, basis)
    one = spectra(width, BLOCKS, lambda spot: (spot,), info, raw_one, raw_basis)

    part = raw_products(width, info, raw_basis, own, one, raw_two)
    first = lax.all_to_all(part, "win", 0, 0, tiled=True, axis_index_groups=turned_groups)
    dealt, part = lax.optimization_barrier((dealt, part))
    second = dealt_products(width, info, dealt_spectra(dealt, basis), *came)
    first, second = lax.optimization_barrier((first, second))
    first = jnp.sum(first.astype(jnp.float32), axis=0).reshape(PCAP, 2, HALF, LENGTH)

    def half(at):
        return jnp.concatenate(
            [
                lax.dynamic_index_in_dim(first, at, axis=1, keepdims=False),
                lax.dynamic_index_in_dim(second, at, axis=0, keepdims=False),
            ],
            axis=1,
        )

    give = half(1 - far).astype(jnp.bfloat16)

    def swapped(slots):
        got = lax.all_gather(give[:slots], "win", axis=0, tiled=True, axis_index_groups=far_groups)
        got = lax.dynamic_slice_in_dim(got, (1 - far) * slots, slots, axis=0).astype(jnp.float32)
        return jnp.concatenate([got, jnp.zeros((PCAP - slots,) + got.shape[1:], jnp.float32)], axis=0)

    got = lax.cond(info[USED + 2] > 0, lambda: swapped(PCAP), lambda: swapped(PCAP // 2))
    return half(far) + got


def local(records, pairs, owner):
    where = lax.axis_index("chan")[None].astype(jnp.int32)
    x = records.reshape(BLOCKS, 16, CHUNKS, HALF, 2, LENGTH)
    narrow, wide, three, deal, *raw = prepare(where, pairs, owner, x)
    return lax.cond(
        three.reshape(()) == 0,
        lambda: path(records, narrow, deal, raw, 2),
        lambda: path(records, wide, deal, None, BLOCKS),
    )


def solution(mesh):
    return jax.shard_map(
        local,
        mesh=mesh,
        in_specs=(P("chan", None, "win", None), P(), P()),
        out_specs=P("chan", "win", None),
        check_vma=False,
    )
```

```python
import math

import jax
import jax.numpy as jnp
import ml_dtypes
import numpy as np
from jax import lax
from jax.experimental import pallas as pl
from jax.experimental.pallas import tpu as pltpu
from jax.sharding import PartitionSpec as P

PCAP = 4
BLOCKS = 3
CHAN = 32
CHUNKS = 2
LENGTH = 1024
BINS = 512
HALF = 16 // CHUNKS
ROWS = 512 // CHUNKS
VMEM = pl.BlockSpec(memory_space=pltpu.VMEM)
SMEM = pl.BlockSpec(memory_space=pltpu.SMEM)
ANY = pl.BlockSpec(memory_space=pl.ANY)
HBM = pl.BlockSpec(memory_space=pltpu.HBM)
PARAMS = pltpu.CompilerParams(vmem_limit_bytes=40 << 20)
ALL_VMEM = pltpu.CompilerParams(vmem_limit_bytes=63 << 20)


def basis_table():
    sample_ids = np.arange(LENGTH, dtype=np.int32)
    bin_ids = np.arange(BINS, dtype=np.int32)
    step = np.float32(2.0 * math.pi / LENGTH)
    phases = (sample_ids[:, None] * bin_ids[None, :] % LENGTH).astype(np.float32) * step
    taper = np.float32(0.5) - np.float32(0.5) * np.cos(sample_ids.astype(np.float32) * step)
    table = np.concatenate([taper[:, None] * np.cos(phases), -taper[:, None] * np.sin(phases)], axis=1)
    return table.astype(ml_dtypes.bfloat16)


LANES, FIRST, SECOND, USED, TABLE = 0, 6, 10, 14, 18
SWAPS = [
    [pair for low in range(start, CHAN - 1, 2) for pair in ((low, low + 1), (low + 1, low))] for start in (1, 0)
]


def fill_tables(where, pairs, owner, narrow, wide, flag, rows):
    odd = where[0] % 2
    me = where[0].astype(jnp.float32)
    count = owner.shape[1]
    rows[...] = jnp.full(rows.shape, -1000.0, jnp.float32)
    rows[0:2, 0:count] = pairs[...].astype(jnp.float32)
    rows[2:3, 0:count] = owner[...].astype(jnp.float32)
    first = rows[0:1, :]
    second = rows[1:2, :]
    holder = rows[2:3, :]

    chan = lax.broadcasted_iota(jnp.int32, (CHAN, 128), 0).astype(jnp.float32)

    def all_three(block, step):
        hits = [
            jnp.max(jnp.where((block == BLOCKS * chan + i) & (holder == chan + step), 1.0, 0.0), axis=1, keepdims=True)
            for i in range(BLOCKS)
        ]
        return hits[0] * hits[1] * hits[2]

    most = jnp.max(jnp.maximum(all_three(first, 1.0), all_three(second, -1.0)))

    def total(hit, value=1.0):
        return jnp.sum(jnp.where(hit, value, 0.0))

    first = first - BLOCKS * me
    second = second - BLOCKS * me
    apart = holder - me
    mine = apart == 0.0

    def needs(hit, block):
        return [(total(hit & (block == float(i))) > 0.0).astype(jnp.int32) for i in range(BLOCKS)]

    to_right = needs(apart == 1.0, first)
    to_left = needs(apart == -1.0, second)
    of_left = needs(mine, first + BLOCKS)
    of_right = needs(mine, second - BLOCKS)
    earlier = lax.broadcasted_iota(jnp.int32, (128, 128), 0) < lax.broadcasted_iota(jnp.int32, (128, 128), 1)
    ranks = jnp.dot(
        jnp.broadcast_to(jnp.where(mine, 1.0, 0.0), (8, 128)).astype(jnp.bfloat16),
        jnp.where(earlier, 1.0, 0.0).astype(jnp.bfloat16),
        preferred_element_type=jnp.float32,
    )[0:1, :]
    number = total(mine).astype(jnp.int32)

    def spot(need, block, width):
        if width == BLOCKS:
            return block
        return jnp.where(block == 0, 0, jnp.where(block == 1, need[0], jnp.minimum(need[0] + need[1], width - 1)))

    def picks(need, width):
        if width == BLOCKS:
            return [jnp.int32(i) for i in range(BLOCKS)]
        n0, n1, n2 = [n > 0 for n in need]
        lowest = jnp.where(n0, 0, jnp.where(n1, 1, jnp.where(n2, 2, 0)))
        after = jnp.where(n0 & n1, 1, jnp.where(n2 & (n0 | n1), 2, lowest))
        return [lowest.astype(jnp.int32), after.astype(jnp.int32), jnp.int32(0)]

    flag[0] = most.astype(jnp.int32)
    for info, width in ((narrow, 2), (wide, BLOCKS)):
        for i, (right, left) in enumerate(zip(picks(to_right, width), picks(to_left, width))):
            info[LANES + i] = jnp.where(odd == 1, right, left)
            info[LANES + 3 + i] = jnp.where(odd == 1, left, right)
    for slot in range(PCAP):
        hit = mine & (ranks == float(slot))
        a = total(hit, first).astype(jnp.int32)
        b = total(hit, second).astype(jnp.int32)
        used = (number > slot).astype(jnp.int32)
        for info, width in ((narrow, 2), (wide, BLOCKS)):
            from_left = BLOCKS + odd * width
            from_right = BLOCKS + (1 - odd) * width
            info[FIRST + slot] = jnp.where(a < 0, from_left + spot(of_left, a + BLOCKS, width), a)
            info[SECOND + slot] = jnp.where(b >= BLOCKS, from_right + spot(of_right, b - BLOCKS, width), b)
            info[USED + slot] = used


def whitened(rows, basis):
    spectrum = jnp.dot(rows, basis, preferred_element_type=jnp.float32)
    power_mean = jnp.mean(spectrum * spectrum, axis=-1, keepdims=True)
    return (spectrum * lax.rsqrt(power_mean + 1e-06)).astype(jnp.bfloat16)


COST = pl.CostEstimate(flops=2 * 3 * ROWS * LENGTH * LENGTH, bytes_accessed=8 << 20, transcendentals=0)


def lane_copy(buf, block, lanes, way, spot, lsem):
    return pltpu.make_async_copy(buf.at[block], lanes[way].at[spot], lsem.at[way, spot])


def start_lanes(width, info, buf, block, lanes, lsem):
    for way in range(2):
        for spot in range(width):

            @pl.when(info[LANES + way * 3 + spot] == block)
            def _(way=way, spot=spot):
                lane_copy(buf, block, lanes, way, spot, lsem).start()


def wait_lanes(width, buf, lanes, lsem):
    for way in range(2):
        for spot in range(width):
            lane_copy(buf, 0, lanes, way, spot, lsem).wait()


def raw_lanes_kernel(width, info, x, one, two, buf, xsem, lsem):
    loads = [pltpu.make_async_copy(x.at[block, :, 0], buf.at[block], xsem.at[block]) for block in range(BLOCKS)]
    for copy in loads:
        copy.start()
    for block, copy in enumerate(loads):
        copy.wait()
        start_lanes(width, info, buf, block, (one, two), lsem)
    wait_lanes(width, buf, (one, two), lsem)


def raw_lanes(width, info, x):
    lane = jax.ShapeDtypeStruct((width, 16, HALF, 2, LENGTH), jnp.bfloat16)
    return pl.pallas_call(
        lambda *refs: raw_lanes_kernel(width, *refs),
        out_shape=(lane, lane),
        in_specs=[SMEM, HBM],
        out_specs=[ANY] * 2,
        scratch_shapes=[
            pltpu.VMEM((BLOCKS, 16, HALF, 2, LENGTH), jnp.bfloat16),
            pltpu.SemaphoreType.DMA((BLOCKS,)),
            pltpu.SemaphoreType.DMA((2, width)),
        ],
        compiler_params=PARAMS,
        cost_estimate=pl.CostEstimate(flops=0, bytes_accessed=4 << 20, transcendentals=0),
        name="raw_lanes",
    )(info, x)


def prepare_kernel(where, pairs, owner, x, narrow, wide, flag, deal, one, two, *scratch):
    pairs_here, owner_here, rows, psem, buf, laid, xsem, dsem, lsem = scratch
    small = [
        pltpu.make_async_copy(pairs, pairs_here, psem.at[0]),
        pltpu.make_async_copy(owner, owner_here, psem.at[1]),
    ]
    for copy in small:
        copy.start()
    loads = [
        [pltpu.make_async_copy(x.at[block, :, chunk], buf.at[chunk, block], xsem.at[chunk, block]) for block in range(BLOCKS)]
        for chunk in range(CHUNKS)
    ]
    for copies in reversed(loads):
        for copy in copies:
            copy.start()
    deals = [
        [
            pltpu.make_async_copy(laid.at[block, z], deal.at[:, block, z], dsem.at[block, z])
            for z in range(2)
        ]
        for block in range(BLOCKS)
    ]
    for block in range(BLOCKS):
        loads[1][block].wait()
        laid[block] = buf[1, block].reshape(2, 8, 2 * HALF, LENGTH)
        for copy in deals[block]:
            copy.start()
    for copy in small:
        copy.wait()
    fill_tables(where, pairs_here, owner_here, narrow, wide, flag, rows)
    for block in range(BLOCKS):
        loads[0][block].wait()
        start_lanes(2, narrow, buf.at[0], block, (one, two), lsem)
    for copies in deals:
        for copy in copies:
            copy.wait()
    wait_lanes(2, buf.at[0], (one, two), lsem)


def prepare(where, pairs, owner, x):
    table = jax.ShapeDtypeStruct((TABLE,), jnp.int32)
    lane = jax.ShapeDtypeStruct((2, 16, HALF, 2, LENGTH), jnp.bfloat16)
    return pl.pallas_call(
        prepare_kernel,
        out_shape=(
            table,
            table,
            jax.ShapeDtypeStruct((1,), jnp.int32),
            jax.ShapeDtypeStruct((8, BLOCKS, 2, 2 * HALF, LENGTH), jnp.bfloat16),
            lane,
            lane,
        ),
        in_specs=[SMEM, HBM, HBM, HBM],
        out_specs=[SMEM] * 3 + [ANY] * 3,
        scratch_shapes=[
            pltpu.VMEM((2, pairs.shape[0]), jnp.int32),
            pltpu.VMEM((1, pairs.shape[0]), jnp.int32),
            pltpu.VMEM((8, 128), jnp.float32),
            pltpu.SemaphoreType.DMA((2,)),
            pltpu.VMEM((CHUNKS, BLOCKS, 16, HALF, 2, LENGTH), jnp.bfloat16),
            pltpu.VMEM((BLOCKS, 2, 8, 2 * HALF, LENGTH), jnp.bfloat16),
            pltpu.SemaphoreType.DMA((CHUNKS, BLOCKS)),
            pltpu.SemaphoreType.DMA((BLOCKS, 2)),
            pltpu.SemaphoreType.DMA((2, 2)),
        ],
        compiler_params=ALL_VMEM,
        cost_estimate=pl.CostEstimate(flops=0, bytes_accessed=7 << 20, transcendentals=0),
        name="prepare",
    )(where, pairs.T, owner[None], x)


def taken(info, spot):
    hits = [
        (info[USED + slot] > 0) & ((info[FIRST + slot] == spot) | (info[SECOND + slot] == spot)) for slot in range(PCAP)
    ]
    return hits[0] | hits[1] | hits[2] | hits[3]


def spectra_kernel(count, base, at, info, x, basis, own, xbuf, spec, xsem, osem):
    def load(block):
        return pltpu.make_async_copy(x.at[at(block)], xbuf.at[block], xsem.at[block])

    def store(block):
        return pltpu.make_async_copy(spec.at[block], own.at[block], osem.at[block])

    for block in range(count):
        load(block).start()
    for block in range(count):
        load(block).wait()

        @pl.when(taken(info, base + block))
        def _(block=block):
            spec[block] = whitened(xbuf[block].reshape(ROWS, LENGTH), basis[...])

        store(block).start()
    for block in range(count):
        store(block).wait()


def spectra(count, base, at, info, x, basis):
    return pl.pallas_call(
        lambda *refs: spectra_kernel(count, base, at, *refs),
        out_shape=jax.ShapeDtypeStruct((count, ROWS, LENGTH), jnp.bfloat16),
        in_specs=[SMEM, HBM, VMEM],
        out_specs=ANY,
        scratch_shapes=[
            pltpu.VMEM((count, 16, HALF, 2, LENGTH), jnp.bfloat16),
            pltpu.VMEM((count, ROWS, LENGTH), jnp.bfloat16),
            pltpu.SemaphoreType.DMA((count,)),
            pltpu.SemaphoreType.DMA((count,)),
        ],
        compiler_params=PARAMS,
        cost_estimate=COST,
        name="spectra",
    )(info, x, basis)


def dealt_kernel(width, info, x, basis, one, two, spec, lsem):
    for block in range(BLOCKS):
        picks = [info[LANES + way * 3 + spot] == block for way in range(2) for spot in range(width)]
        wanted = picks[0]
        for pick in picks[1:]:
            wanted = wanted | pick

        @pl.when(wanted)
        def _(block=block):
            spec[block] = whitened(x[:, block].reshape(ROWS, LENGTH), basis[...])
            start_lanes(width, info, spec, block, (one, two), lsem)

    wait_lanes(width, spec, (one, two), lsem)


def dealt_lanes(width, info, x, basis):
    lane = jax.ShapeDtypeStruct((width, ROWS, LENGTH), jnp.bfloat16)
    return pl.pallas_call(
        lambda *refs: dealt_kernel(width, *refs),
        out_shape=(lane, lane),
        in_specs=[SMEM, VMEM, VMEM],
        out_specs=[HBM] * 2,
        scratch_shapes=[
            pltpu.VMEM((BLOCKS, ROWS, LENGTH), jnp.bfloat16),
            pltpu.SemaphoreType.DMA((2, width)),
        ],
        compiler_params=PARAMS,
        cost_estimate=COST,
        name="dealt_lanes",
    )(info, x, basis)


def dealt_own_kernel(x, basis, own):
    for block in range(BLOCKS):
        own[block] = whitened(x[:, block].reshape(ROWS, LENGTH), basis[...])


def dealt_spectra(x, basis):
    return pl.pallas_call(
        dealt_own_kernel,
        out_shape=jax.ShapeDtypeStruct((BLOCKS, ROWS, LENGTH), jnp.bfloat16),
        in_specs=[VMEM, VMEM],
        out_specs=VMEM,
        compiler_params=PARAMS,
        cost_estimate=COST,
        name="dealt_spectra",
    )(x, basis)


def parts(read, at, lane):
    a_re, a_im, b_re, b_im = [
        read(operand, at, pl.ds(start + lane * 128, 128)).astype(jnp.float32)
        for operand in range(2)
        for start in (0, BINS)
    ]
    return a_re * b_re + a_im * b_im, a_im * b_re - a_re * b_im


def pair_sums(acc):
    return acc[pl.ds(0, HALF, 2), :] + acc[pl.ds(1, HALF, 2), :]


def tile(index):
    return pl.ds(pl.multiple_of(index * 2 * HALF, 2 * HALF), 2 * HALF)


def raw_products_kernel(width, info, basis, own, one, two, out, xbuf, buf, acc, xsem, osem):
    loads = [pltpu.make_async_copy(two.at[spot], xbuf.at[spot], xsem.at[spot]) for spot in range(width)]
    ready = [
        pltpu.make_async_copy(own, buf.at[pl.ds(0, BLOCKS)], osem.at[0]),
        pltpu.make_async_copy(one, buf.at[pl.ds(BLOCKS, width)], osem.at[1]),
    ]
    for copy in loads + ready:
        copy.start()
    for spot, copy in enumerate(loads):
        copy.wait()

        @pl.when(taken(info, BLOCKS + width + spot))
        def _(spot=spot):
            buf[BLOCKS + width + spot] = whitened(xbuf[spot].reshape(ROWS, LENGTH), basis[...])

    for copy in ready:
        copy.wait()

    @pl.loop(0, PCAP)
    def _(slot):
        spots = info[FIRST + slot], info[SECOND + slot]

        def read(operand, at, part):
            return buf[spots[operand], at, part]

        @pl.when(info[USED + slot] > 0)
        def _():
            @pl.loop(0, 8)
            def _(peer):
                for lane in range(BINS // 128):
                    for z in range(2):
                        acc[lane, z, 0], acc[lane, z, 1] = parts(read, tile(z * 8 + (peer + 4) % 8), lane)
                    for part in range(2):
                        sums = [pair_sums(acc.at[lane, z, part]) for z in range(2)]
                        out[peer, slot, :, pl.ds(part * BINS + lane * 128, 128)] = jnp.concatenate(
                            sums, axis=0
                        ).astype(jnp.bfloat16)

        @pl.when(info[USED + slot] == 0)
        def _():
            @pl.loop(0, 8)
            def _(peer):
                out[peer, slot] = jnp.zeros((2 * HALF, LENGTH), jnp.bfloat16)


def raw_products(width, info, basis, own, one, two):
    return pl.pallas_call(
        lambda *refs: raw_products_kernel(width, *refs),
        out_shape=jax.ShapeDtypeStruct((8, PCAP, 2 * HALF, LENGTH), jnp.bfloat16),
        in_specs=[SMEM, VMEM, ANY, ANY, HBM],
        out_specs=VMEM,
        scratch_shapes=[
            pltpu.VMEM((width, 16, HALF, 2, LENGTH), jnp.bfloat16),
            pltpu.VMEM((BLOCKS + 2 * width, ROWS, LENGTH), jnp.bfloat16),
            pltpu.VMEM((BINS // 128, 2, 2, 2 * HALF, 128), jnp.float32),
            pltpu.SemaphoreType.DMA((width,)),
            pltpu.SemaphoreType.DMA((2,)),
        ],
        compiler_params=PARAMS,
        cost_estimate=COST,
        name="raw_products",
    )(info, basis, own, one, two)


def dealt_products_kernel(width, info, own, one, two, out, buf, acc, sems):
    def start(slot, operand, spot):
        to, sem = buf.at[slot, operand], sems.at[slot, operand]

        @pl.when(spot < BLOCKS)
        def _():
            pltpu.make_async_copy(own.at[spot], to, sem).start()

        @pl.when((spot >= BLOCKS) & (spot < BLOCKS + width))
        def _():
            pltpu.make_async_copy(one.at[spot - BLOCKS], to, sem).start()

        @pl.when(spot >= BLOCKS + width)
        def _():
            pltpu.make_async_copy(two.at[spot - BLOCKS - width], to, sem).start()

    for slot in range(PCAP):

        @pl.when(info[USED + slot] > 0)
        def _(slot=slot):
            start(slot, 0, info[FIRST + slot])
            start(slot, 1, info[SECOND + slot])

    @pl.loop(0, PCAP)
    def _(slot):
        def read(operand, at, part):
            return buf[slot, operand, at, part]

        @pl.when(info[USED + slot] > 0)
        def _():
            for operand in range(2):
                pltpu.make_async_copy(own.at[0], buf.at[slot, operand], sems.at[slot, operand]).wait()

            @pl.loop(0, 2)
            def _(z):
                for lane in range(BINS // 128):
                    real, imag = parts(read, tile(z), lane)
                    for source in range(1, 8):
                        re, im = parts(read, tile(source * 2 + z), lane)
                        real, imag = real + re, imag + im
                    acc[lane, 0], acc[lane, 1] = real, imag
                    for part in range(2):
                        out[z, slot, :, pl.ds(part * BINS + lane * 128, 128)] = pair_sums(acc.at[lane, part])

        @pl.when(info[USED + slot] == 0)
        def _():
            for z in range(2):
                out[z, slot] = jnp.zeros((HALF, LENGTH), jnp.float32)


def dealt_products(width, info, own, one, two):
    return pl.pallas_call(
        lambda *refs: dealt_products_kernel(width, *refs),
        out_shape=jax.ShapeDtypeStruct((2, PCAP, HALF, LENGTH), jnp.float32),
        in_specs=[SMEM] + [ANY] * 3,
        out_specs=VMEM,
        scratch_shapes=[
            pltpu.VMEM((PCAP, 2, ROWS, LENGTH), jnp.bfloat16),
            pltpu.VMEM((BINS // 128, 2, 2 * HALF, 128), jnp.float32),
            pltpu.SemaphoreType.DMA((PCAP, 2)),
        ],
        compiler_params=PARAMS,
        cost_estimate=pl.CostEstimate(flops=1 << 25, bytes_accessed=8 << 20, transcendentals=0),
        name="dealt_products",
    )(info, own, one, two)


def path(records, info, deal, raw, width):
    far = lax.axis_index("win") // 8
    basis = jnp.asarray(basis_table())
    x = records.reshape(BLOCKS, 16, CHUNKS, HALF, 2, LENGTH)
    chip_groups = [[z * 8 + j for j in range(8)] for z in range(2)]
    turned_groups = [[z * 8 + (j + 4) % 8 for j in range(8)] for z in range(2)]
    far_groups = [[z * 8 + j for z in range(2)] for j in range(8)]

    dealt = lax.all_to_all(deal, "win", 0, 0, tiled=True, axis_index_groups=chip_groups)
    if raw is None:
        raw = raw_lanes(width, info, x)
    raw_one, raw_two = [lax.ppermute(lane, "chan", swap) for lane, swap in zip(raw, SWAPS)]
    sent = dealt_lanes(width, info, dealt, basis)
    raw_basis, *sent = lax.optimization_barrier((basis, *sent))
    came = [lax.ppermute(lane, "chan", swap) for lane, swap in zip(sent, SWAPS)]
    own = spectra(BLOCKS, 0, lambda block: (block, slice(None), 0), info, x, basis)
    one = spectra(width, BLOCKS, lambda spot: (spot,), info, raw_one, raw_basis)

    part = raw_products(width, info, raw_basis, own, one, raw_two)
    first = lax.all_to_all(part, "win", 0, 0, tiled=True, axis_index_groups=turned_groups)
    dealt, part = lax.optimization_barrier((dealt, part))
    second = dealt_products(width, info, dealt_spectra(dealt, basis), *came)
    first, second = lax.optimization_barrier((first, second))
    first = jnp.sum(first.astype(jnp.float32), axis=0).reshape(PCAP, 2, HALF, LENGTH)

    def half(at):
        return jnp.concatenate(
            [
                lax.dynamic_index_in_dim(first, at, axis=1, keepdims=False),
                lax.dynamic_index_in_dim(second, at, axis=0, keepdims=False),
            ],
            axis=1,
        )

    give = half(1 - far).astype(jnp.bfloat16)

    def swapped(slots):
        got = lax.all_gather(give[:slots], "win", axis=0, tiled=True, axis_index_groups=far_groups)
        got = lax.dynamic_slice_in_dim(got, (1 - far) * slots, slots, axis=0).astype(jnp.float32)
        return jnp.concatenate([got, jnp.zeros((PCAP - slots,) + got.shape[1:], jnp.float32)], axis=0)

    got = lax.cond(info[USED + 2] > 0, lambda: swapped(PCAP), lambda: swapped(PCAP // 2))
    return half(far) + got


def local(records, pairs, owner):
    where = lax.axis_index("chan")[None].astype(jnp.int32)
    x = records.reshape(BLOCKS, 16, CHUNKS, HALF, 2, LENGTH)
    narrow, wide, three, deal, *raw = prepare(where, pairs, owner, x)
    return lax.cond(
        three.reshape(()) == 0,
        lambda: path(records, narrow, deal, raw, 2),
        lambda: path(records, wide, deal, None, BLOCKS),
    )


def solution(mesh):
    return jax.shard_map(
        local,
        mesh=mesh,
        in_specs=(P("chan", None, "win", None), P(), P()),
        out_specs=P("chan", "win", None),
        check_vma=False,
    )
```

```python
import math

import jax
import jax.numpy as jnp
import ml_dtypes
import numpy as np
from jax import lax
from jax.experimental import pallas as pl
from jax.experimental.pallas import tpu as pltpu
from jax.sharding import PartitionSpec as P

PCAP = 4
BLOCKS = 3
CHAN = 32
CHUNKS = 2
LENGTH = 1024
BINS = 512
HALF = 16 // CHUNKS
ROWS = 512 // CHUNKS
VMEM = pl.BlockSpec(memory_space=pltpu.VMEM)
SMEM = pl.BlockSpec(memory_space=pltpu.SMEM)
ANY = pl.BlockSpec(memory_space=pl.ANY)
HBM = pl.BlockSpec(memory_space=pltpu.HBM)
PARAMS = pltpu.CompilerParams(vmem_limit_bytes=40 << 20)
ALL_VMEM = pltpu.CompilerParams(vmem_limit_bytes=63 << 20)


def basis_table():
    sample_ids = np.arange(LENGTH, dtype=np.int32)
    bin_ids = np.arange(BINS, dtype=np.int32)
    step = np.float32(2.0 * math.pi / LENGTH)
    phases = (sample_ids[:, None] * bin_ids[None, :] % LENGTH).astype(np.float32) * step
    taper = np.float32(0.5) - np.float32(0.5) * np.cos(sample_ids.astype(np.float32) * step)
    table = np.concatenate([taper[:, None] * np.cos(phases), -taper[:, None] * np.sin(phases)], axis=1)
    return table.astype(ml_dtypes.bfloat16)


LANES, FIRST, SECOND, USED, TABLE = 0, 6, 10, 14, 18
SWAPS = [
    [pair for low in range(start, CHAN - 1, 2) for pair in ((low, low + 1), (low + 1, low))] for start in (1, 0)
]


def fill_tables(where, pairs, owner, narrow, wide, flag, rows):
    odd = where[0] % 2
    me = where[0].astype(jnp.float32)
    count = owner.shape[1]
    rows[...] = jnp.full(rows.shape, -1000.0, jnp.float32)
    rows[0:2, 0:count] = pairs[...].astype(jnp.float32)
    rows[2:3, 0:count] = owner[...].astype(jnp.float32)
    first = rows[0:1, :]
    second = rows[1:2, :]
    holder = rows[2:3, :]

    chan = lax.broadcasted_iota(jnp.int32, (CHAN, 128), 0).astype(jnp.float32)

    def all_three(block, step):
        hits = [
            jnp.max(jnp.where((block == BLOCKS * chan + i) & (holder == chan + step), 1.0, 0.0), axis=1, keepdims=True)
            for i in range(BLOCKS)
        ]
        return hits[0] * hits[1] * hits[2]

    most = jnp.max(jnp.maximum(all_three(first, 1.0), all_three(second, -1.0)))

    def total(hit, value=1.0):
        return jnp.sum(jnp.where(hit, value, 0.0))

    first = first - BLOCKS * me
    second = second - BLOCKS * me
    apart = holder - me
    mine = apart == 0.0

    def needs(hit, block):
        return [(total(hit & (block == float(i))) > 0.0).astype(jnp.int32) for i in range(BLOCKS)]

    to_right = needs(apart == 1.0, first)
    to_left = needs(apart == -1.0, second)
    of_left = needs(mine, first + BLOCKS)
    of_right = needs(mine, second - BLOCKS)
    earlier = lax.broadcasted_iota(jnp.int32, (128, 128), 0) < lax.broadcasted_iota(jnp.int32, (128, 128), 1)
    ranks = jnp.dot(
        jnp.broadcast_to(jnp.where(mine, 1.0, 0.0), (8, 128)).astype(jnp.bfloat16),
        jnp.where(earlier, 1.0, 0.0).astype(jnp.bfloat16),
        preferred_element_type=jnp.float32,
    )[0:1, :]
    number = total(mine).astype(jnp.int32)

    def spot(need, block, width):
        if width == BLOCKS:
            return block
        return jnp.where(block == 0, 0, jnp.where(block == 1, need[0], jnp.minimum(need[0] + need[1], width - 1)))

    def picks(need, width):
        if width == BLOCKS:
            return [jnp.int32(i) for i in range(BLOCKS)]
        n0, n1, n2 = [n > 0 for n in need]
        lowest = jnp.where(n0, 0, jnp.where(n1, 1, jnp.where(n2, 2, 0)))
        after = jnp.where(n0 & n1, 1, jnp.where(n2 & (n0 | n1), 2, lowest))
        return [lowest.astype(jnp.int32), after.astype(jnp.int32), jnp.int32(0)]

    flag[0] = most.astype(jnp.int32)
    for info, width in ((narrow, 2), (wide, BLOCKS)):
        for i, (right, left) in enumerate(zip(picks(to_right, width), picks(to_left, width))):
            info[LANES + i] = jnp.where(odd == 1, right, left)
            info[LANES + 3 + i] = jnp.where(odd == 1, left, right)
    for slot in range(PCAP):
        hit = mine & (ranks == float(slot))
        a = total(hit, first).astype(jnp.int32)
        b = total(hit, second).astype(jnp.int32)
        used = (number > slot).astype(jnp.int32)
        for info, width in ((narrow, 2), (wide, BLOCKS)):
            from_left = BLOCKS + odd * width
            from_right = BLOCKS + (1 - odd) * width
            info[FIRST + slot] = jnp.where(a < 0, from_left + spot(of_left, a + BLOCKS, width), a)
            info[SECOND + slot] = jnp.where(b >= BLOCKS, from_right + spot(of_right, b - BLOCKS, width), b)
            info[USED + slot] = used


def whitened(rows, basis):
    spectrum = jnp.dot(rows, basis, preferred_element_type=jnp.float32)
    power_mean = jnp.mean(spectrum * spectrum, axis=-1, keepdims=True)
    return (spectrum * lax.rsqrt(power_mean + 1e-06)).astype(jnp.bfloat16)


COST = pl.CostEstimate(flops=2 * 3 * ROWS * LENGTH * LENGTH, bytes_accessed=8 << 20, transcendentals=0)


def lane_copy(buf, block, lanes, way, spot, lsem):
    return pltpu.make_async_copy(buf.at[block], lanes[way].at[spot], lsem.at[way, spot])


def start_lanes(width, info, buf, block, lanes, lsem):
    for way in range(2):
        for spot in range(width):

            @pl.when(info[LANES + way * 3 + spot] == block)
            def _(way=way, spot=spot):
                lane_copy(buf, block, lanes, way, spot, lsem).start()


def wait_lanes(width, buf, lanes, lsem):
    for way in range(2):
        for spot in range(width):
            lane_copy(buf, 0, lanes, way, spot, lsem).wait()


def raw_lanes_kernel(width, info, x, one, two, buf, plain, xsem, lsem):
    loads = [pltpu.make_async_copy(x.at[block, :, 0], buf.at[block], xsem.at[block]) for block in range(BLOCKS)]
    for copy in loads:
        copy.start()
    for block, copy in enumerate(loads):
        copy.wait()
        plain[block] = buf[block].reshape(ROWS, LENGTH)
        start_lanes(width, info, plain, block, (one, two), lsem)
    wait_lanes(width, plain, (one, two), lsem)


def raw_lanes(width, info, x):
    lane = jax.ShapeDtypeStruct((width, ROWS, LENGTH), jnp.bfloat16)
    return pl.pallas_call(
        lambda *refs: raw_lanes_kernel(width, *refs),
        out_shape=(lane, lane),
        in_specs=[SMEM, HBM],
        out_specs=[ANY] * 2,
        scratch_shapes=[
            pltpu.VMEM((BLOCKS, 16, HALF, 2, LENGTH), jnp.bfloat16),
            pltpu.VMEM((BLOCKS, ROWS, LENGTH), jnp.bfloat16),
            pltpu.SemaphoreType.DMA((BLOCKS,)),
            pltpu.SemaphoreType.DMA((2, width)),
        ],
        compiler_params=PARAMS,
        cost_estimate=pl.CostEstimate(flops=0, bytes_accessed=4 << 20, transcendentals=0),
        name="raw_lanes",
    )(info, x)


def prepare_kernel(where, pairs, owner, x, narrow, wide, flag, deal, one, two, *scratch):
    pairs_here, owner_here, rows, psem, buf, laid, plain, xsem, dsem, lsem = scratch
    small = [
        pltpu.make_async_copy(pairs, pairs_here, psem.at[0]),
        pltpu.make_async_copy(owner, owner_here, psem.at[1]),
    ]
    for copy in small:
        copy.start()
    loads = [
        [pltpu.make_async_copy(x.at[block, :, chunk], buf.at[chunk, block], xsem.at[chunk, block]) for block in range(BLOCKS)]
        for chunk in range(CHUNKS)
    ]
    for copies in reversed(loads):
        for copy in copies:
            copy.start()
    deals = [
        [
            pltpu.make_async_copy(laid.at[block, z], deal.at[:, block, z], dsem.at[block, z])
            for z in range(2)
        ]
        for block in range(BLOCKS)
    ]
    for block in range(BLOCKS):
        loads[1][block].wait()
        laid[block] = buf[1, block].reshape(2, 8, 2 * HALF, LENGTH)
        for copy in deals[block]:
            copy.start()
    for copy in small:
        copy.wait()
    fill_tables(where, pairs_here, owner_here, narrow, wide, flag, rows)
    for block in range(BLOCKS):
        loads[0][block].wait()
        plain[block] = buf[0, block].reshape(ROWS, LENGTH)
        start_lanes(2, narrow, plain, block, (one, two), lsem)
    for copies in deals:
        for copy in copies:
            copy.wait()
    wait_lanes(2, plain, (one, two), lsem)


def prepare(where, pairs, owner, x):
    table = jax.ShapeDtypeStruct((TABLE,), jnp.int32)
    lane = jax.ShapeDtypeStruct((2, ROWS, LENGTH), jnp.bfloat16)
    return pl.pallas_call(
        prepare_kernel,
        out_shape=(
            table,
            table,
            jax.ShapeDtypeStruct((1,), jnp.int32),
            jax.ShapeDtypeStruct((8, BLOCKS, 2, 2 * HALF, LENGTH), jnp.bfloat16),
            lane,
            lane,
        ),
        in_specs=[SMEM, HBM, HBM, HBM],
        out_specs=[SMEM] * 3 + [ANY] * 3,
        scratch_shapes=[
            pltpu.VMEM((2, pairs.shape[0]), jnp.int32),
            pltpu.VMEM((1, pairs.shape[0]), jnp.int32),
            pltpu.VMEM((8, 128), jnp.float32),
            pltpu.SemaphoreType.DMA((2,)),
            pltpu.VMEM((CHUNKS, BLOCKS, 16, HALF, 2, LENGTH), jnp.bfloat16),
            pltpu.VMEM((BLOCKS, 2, 8, 2 * HALF, LENGTH), jnp.bfloat16),
            pltpu.VMEM((BLOCKS, ROWS, LENGTH), jnp.bfloat16),
            pltpu.SemaphoreType.DMA((CHUNKS, BLOCKS)),
            pltpu.SemaphoreType.DMA((BLOCKS, 2)),
            pltpu.SemaphoreType.DMA((2, 2)),
        ],
        compiler_params=ALL_VMEM,
        cost_estimate=pl.CostEstimate(flops=0, bytes_accessed=7 << 20, transcendentals=0),
        name="prepare",
    )(where, pairs.T, owner[None], x)


def taken(info, spot):
    hits = [
        (info[USED + slot] > 0) & ((info[FIRST + slot] == spot) | (info[SECOND + slot] == spot)) for slot in range(PCAP)
    ]
    return hits[0] | hits[1] | hits[2] | hits[3]


def spectra_kernel(count, base, at, info, x, basis, own, xbuf, spec, xsem, osem):
    def load(block):
        return pltpu.make_async_copy(x.at[at(block)], xbuf.at[block], xsem.at[block])

    def store(block):
        return pltpu.make_async_copy(spec.at[block], own.at[block], osem.at[block])

    for block in range(count):
        load(block).start()
    for block in range(count):
        load(block).wait()

        @pl.when(taken(info, base + block))
        def _(block=block):
            spec[block] = whitened(xbuf[block].reshape(ROWS, LENGTH), basis[...])

        store(block).start()
    for block in range(count):
        store(block).wait()


def spectra(count, base, at, shape, info, x, basis):
    return pl.pallas_call(
        lambda *refs: spectra_kernel(count, base, at, *refs),
        out_shape=jax.ShapeDtypeStruct((count, ROWS, LENGTH), jnp.bfloat16),
        in_specs=[SMEM, HBM, VMEM],
        out_specs=ANY,
        scratch_shapes=[
            pltpu.VMEM((count,) + shape, jnp.bfloat16),
            pltpu.VMEM((count, ROWS, LENGTH), jnp.bfloat16),
            pltpu.SemaphoreType.DMA((count,)),
            pltpu.SemaphoreType.DMA((count,)),
        ],
        compiler_params=PARAMS,
        cost_estimate=COST,
        name="spectra",
    )(info, x, basis)


def dealt_kernel(width, info, x, basis, one, two, spec, lsem):
    for block in range(BLOCKS):
        picks = [info[LANES + way * 3 + spot] == block for way in range(2) for spot in range(width)]
        wanted = picks[0]
        for pick in picks[1:]:
            wanted = wanted | pick

        @pl.when(wanted)
        def _(block=block):
            spec[block] = whitened(x[:, block].reshape(ROWS, LENGTH), basis[...])
            start_lanes(width, info, spec, block, (one, two), lsem)

    wait_lanes(width, spec, (one, two), lsem)


def dealt_lanes(width, info, x, basis):
    lane = jax.ShapeDtypeStruct((width, ROWS, LENGTH), jnp.bfloat16)
    return pl.pallas_call(
        lambda *refs: dealt_kernel(width, *refs),
        out_shape=(lane, lane),
        in_specs=[SMEM, VMEM, VMEM],
        out_specs=[HBM] * 2,
        scratch_shapes=[
            pltpu.VMEM((BLOCKS, ROWS, LENGTH), jnp.bfloat16),
            pltpu.SemaphoreType.DMA((2, width)),
        ],
        compiler_params=PARAMS,
        cost_estimate=COST,
        name="dealt_lanes",
    )(info, x, basis)


def dealt_own_kernel(x, basis, own):
    for block in range(BLOCKS):
        own[block] = whitened(x[:, block].reshape(ROWS, LENGTH), basis[...])


def dealt_spectra(x, basis):
    return pl.pallas_call(
        dealt_own_kernel,
        out_shape=jax.ShapeDtypeStruct((BLOCKS, ROWS, LENGTH), jnp.bfloat16),
        in_specs=[VMEM, VMEM],
        out_specs=VMEM,
        compiler_params=PARAMS,
        cost_estimate=COST,
        name="dealt_spectra",
    )(x, basis)


def parts(read, at, lane):
    a_re, a_im, b_re, b_im = [
        read(operand, at, pl.ds(start + lane * 128, 128)).astype(jnp.float32)
        for operand in range(2)
        for start in (0, BINS)
    ]
    return a_re * b_re + a_im * b_im, a_im * b_re - a_re * b_im


def pair_sums(acc):
    return acc[pl.ds(0, HALF, 2), :] + acc[pl.ds(1, HALF, 2), :]


def tile(index):
    return pl.ds(pl.multiple_of(index * 2 * HALF, 2 * HALF), 2 * HALF)


def raw_products_kernel(width, info, basis, own, one, two, out, xbuf, buf, acc, xsem, osem):
    loads = [pltpu.make_async_copy(two.at[spot], xbuf.at[spot], xsem.at[spot]) for spot in range(width)]
    ready = [
        pltpu.make_async_copy(own, buf.at[pl.ds(0, BLOCKS)], osem.at[0]),
        pltpu.make_async_copy(one, buf.at[pl.ds(BLOCKS, width)], osem.at[1]),
    ]
    for copy in loads + ready:
        copy.start()
    for spot, copy in enumerate(loads):
        copy.wait()

        @pl.when(taken(info, BLOCKS + width + spot))
        def _(spot=spot):
            buf[BLOCKS + width + spot] = whitened(xbuf[spot].reshape(ROWS, LENGTH), basis[...])

    for copy in ready:
        copy.wait()

    @pl.loop(0, PCAP)
    def _(slot):
        spots = info[FIRST + slot], info[SECOND + slot]

        def read(operand, at, part):
            return buf[spots[operand], at, part]

        @pl.when(info[USED + slot] > 0)
        def _():
            @pl.loop(0, 8)
            def _(peer):
                for lane in range(BINS // 128):
                    for z in range(2):
                        acc[lane, z, 0], acc[lane, z, 1] = parts(read, tile(z * 8 + (peer + 4) % 8), lane)
                    for part in range(2):
                        sums = [pair_sums(acc.at[lane, z, part]) for z in range(2)]
                        out[peer, slot, :, pl.ds(part * BINS + lane * 128, 128)] = jnp.concatenate(
                            sums, axis=0
                        ).astype(jnp.bfloat16)

        @pl.when(info[USED + slot] == 0)
        def _():
            @pl.loop(0, 8)
            def _(peer):
                out[peer, slot] = jnp.zeros((2 * HALF, LENGTH), jnp.bfloat16)


def raw_products(width, info, basis, own, one, two):
    return pl.pallas_call(
        lambda *refs: raw_products_kernel(width, *refs),
        out_shape=jax.ShapeDtypeStruct((8, PCAP, 2 * HALF, LENGTH), jnp.bfloat16),
        in_specs=[SMEM, VMEM, ANY, ANY, HBM],
        out_specs=VMEM,
        scratch_shapes=[
            pltpu.VMEM((width, ROWS, LENGTH), jnp.bfloat16),
            pltpu.VMEM((BLOCKS + 2 * width, ROWS, LENGTH), jnp.bfloat16),
            pltpu.VMEM((BINS // 128, 2, 2, 2 * HALF, 128), jnp.float32),
            pltpu.SemaphoreType.DMA((width,)),
            pltpu.SemaphoreType.DMA((2,)),
        ],
        compiler_params=PARAMS,
        cost_estimate=COST,
        name="raw_products",
    )(info, basis, own, one, two)


def dealt_products_kernel(width, info, own, one, two, out, buf, acc, sems):
    def start(slot, operand, spot):
        to, sem = buf.at[slot, operand], sems.at[slot, operand]

        @pl.when(spot < BLOCKS)
        def _():
            pltpu.make_async_copy(own.at[spot], to, sem).start()

        @pl.when((spot >= BLOCKS) & (spot < BLOCKS + width))
        def _():
            pltpu.make_async_copy(one.at[spot - BLOCKS], to, sem).start()

        @pl.when(spot >= BLOCKS + width)
        def _():
            pltpu.make_async_copy(two.at[spot - BLOCKS - width], to, sem).start()

    for slot in range(PCAP):

        @pl.when(info[USED + slot] > 0)
        def _(slot=slot):
            start(slot, 0, info[FIRST + slot])
            start(slot, 1, info[SECOND + slot])

    @pl.loop(0, PCAP)
    def _(slot):
        def read(operand, at, part):
            return buf[slot, operand, at, part]

        @pl.when(info[USED + slot] > 0)
        def _():
            for operand in range(2):
                pltpu.make_async_copy(own.at[0], buf.at[slot, operand], sems.at[slot, operand]).wait()

            @pl.loop(0, 2)
            def _(z):
                for lane in range(BINS // 128):
                    real, imag = parts(read, tile(z), lane)
                    for source in range(1, 8):
                        re, im = parts(read, tile(source * 2 + z), lane)
                        real, imag = real + re, imag + im
                    acc[lane, 0], acc[lane, 1] = real, imag
                    for part in range(2):
                        out[z, slot, :, pl.ds(part * BINS + lane * 128, 128)] = pair_sums(acc.at[lane, part])

        @pl.when(info[USED + slot] == 0)
        def _():
            for z in range(2):
                out[z, slot] = jnp.zeros((HALF, LENGTH), jnp.float32)


def dealt_products(width, info, own, one, two):
    return pl.pallas_call(
        lambda *refs: dealt_products_kernel(width, *refs),
        out_shape=jax.ShapeDtypeStruct((2, PCAP, HALF, LENGTH), jnp.float32),
        in_specs=[SMEM] + [ANY] * 3,
        out_specs=VMEM,
        scratch_shapes=[
            pltpu.VMEM((PCAP, 2, ROWS, LENGTH), jnp.bfloat16),
            pltpu.VMEM((BINS // 128, 2, 2 * HALF, 128), jnp.float32),
            pltpu.SemaphoreType.DMA((PCAP, 2)),
        ],
        compiler_params=PARAMS,
        cost_estimate=pl.CostEstimate(flops=1 << 25, bytes_accessed=8 << 20, transcendentals=0),
        name="dealt_products",
    )(info, own, one, two)


def path(records, info, deal, raw, width):
    far = lax.axis_index("win") // 8
    basis = jnp.asarray(basis_table())
    x = records.reshape(BLOCKS, 16, CHUNKS, HALF, 2, LENGTH)
    chip_groups = [[z * 8 + j for j in range(8)] for z in range(2)]
    turned_groups = [[z * 8 + (j + 4) % 8 for j in range(8)] for z in range(2)]
    far_groups = [[z * 8 + j for z in range(2)] for j in range(8)]

    dealt = lax.all_to_all(deal, "win", 0, 0, tiled=True, axis_index_groups=chip_groups)
    if raw is None:
        raw = raw_lanes(width, info, x)
    raw_one, raw_two = [lax.ppermute(lane, "chan", swap) for lane, swap in zip(raw, SWAPS)]
    sent = dealt_lanes(width, info, dealt, basis)
    raw_basis, *sent = lax.optimization_barrier((basis, *sent))
    came = [lax.ppermute(lane, "chan", swap) for lane, swap in zip(sent, SWAPS)]
    own = spectra(BLOCKS, 0, lambda block: (block, slice(None), 0), (16, HALF, 2, LENGTH), info, x, basis)
    one = spectra(width, BLOCKS, lambda spot: (spot,), (ROWS, LENGTH), info, raw_one, raw_basis)

    part = raw_products(width, info, raw_basis, own, one, raw_two)
    first = lax.all_to_all(part, "win", 0, 0, tiled=True, axis_index_groups=turned_groups)
    dealt, part = lax.optimization_barrier((dealt, part))
    second = dealt_products(width, info, dealt_spectra(dealt, basis), *came)
    first, second = lax.optimization_barrier((first, second))
    first = jnp.sum(first.astype(jnp.float32), axis=0).reshape(PCAP, 2, HALF, LENGTH)

    def half(at):
        return jnp.concatenate(
            [
                lax.dynamic_index_in_dim(first, at, axis=1, keepdims=False),
                lax.dynamic_index_in_dim(second, at, axis=0, keepdims=False),
            ],
            axis=1,
        )

    give = half(1 - far).astype(jnp.bfloat16)

    def swapped(slots):
        got = lax.all_gather(give[:slots], "win", axis=0, tiled=True, axis_index_groups=far_groups)
        got = lax.dynamic_slice_in_dim(got, (1 - far) * slots, slots, axis=0).astype(jnp.float32)
        return jnp.concatenate([got, jnp.zeros((PCAP - slots,) + got.shape[1:], jnp.float32)], axis=0)

    got = lax.cond(info[USED + 2] > 0, lambda: swapped(PCAP), lambda: swapped(PCAP // 2))
    return half(far) + got


def local(records, pairs, owner):
    where = lax.axis_index("chan")[None].astype(jnp.int32)
    x = records.reshape(BLOCKS, 16, CHUNKS, HALF, 2, LENGTH)
    narrow, wide, three, deal, *raw = prepare(where, pairs, owner, x)
    return lax.cond(
        three.reshape(()) == 0,
        lambda: path(records, narrow, deal, raw, 2),
        lambda: path(records, wide, deal, None, BLOCKS),
    )


def solution(mesh):
    return jax.shard_map(
        local,
        mesh=mesh,
        in_specs=(P("chan", None, "win", None), P(), P()),
        out_specs=P("chan", "win", None),
        check_vma=False,
    )
```

```python
import math

import jax
import jax.numpy as jnp
import ml_dtypes
import numpy as np
from jax import lax
from jax.experimental import pallas as pl
from jax.experimental.pallas import tpu as pltpu
from jax.sharding import PartitionSpec as P

PCAP = 4
BLOCKS = 3
CHAN = 32
CHUNKS = 2
LENGTH = 1024
BINS = 512
HALF = 16 // CHUNKS
ROWS = 512 // CHUNKS
VMEM = pl.BlockSpec(memory_space=pltpu.VMEM)
SMEM = pl.BlockSpec(memory_space=pltpu.SMEM)
ANY = pl.BlockSpec(memory_space=pl.ANY)
HBM = pl.BlockSpec(memory_space=pltpu.HBM)
PARAMS = pltpu.CompilerParams(vmem_limit_bytes=40 << 20)
ALL_VMEM = pltpu.CompilerParams(vmem_limit_bytes=63 << 20)


def basis_table():
    sample_ids = np.arange(LENGTH, dtype=np.int32)
    bin_ids = np.arange(BINS, dtype=np.int32)
    step = np.float32(2.0 * math.pi / LENGTH)
    phases = (sample_ids[:, None] * bin_ids[None, :] % LENGTH).astype(np.float32) * step
    taper = np.float32(0.5) - np.float32(0.5) * np.cos(sample_ids.astype(np.float32) * step)
    table = np.concatenate([taper[:, None] * np.cos(phases), -taper[:, None] * np.sin(phases)], axis=1)
    return table.astype(ml_dtypes.bfloat16)


LANES, FIRST, SECOND, USED, TABLE = 0, 6, 10, 14, 18
SWAPS = [
    [pair for low in range(start, CHAN - 1, 2) for pair in ((low, low + 1), (low + 1, low))] for start in (1, 0)
]


def fill_tables(where, pairs, owner, narrow, wide, flag, rows):
    odd = where[0] % 2
    me = where[0].astype(jnp.float32)
    count = owner.shape[1]
    rows[...] = jnp.full(rows.shape, -1000.0, jnp.float32)
    rows[0:2, 0:count] = pairs[...].astype(jnp.float32)
    rows[2:3, 0:count] = owner[...].astype(jnp.float32)
    first = rows[0:1, :]
    second = rows[1:2, :]
    holder = rows[2:3, :]

    chan = lax.broadcasted_iota(jnp.int32, (CHAN, 128), 0).astype(jnp.float32)

    def all_three(block, step):
        hits = [
            jnp.max(jnp.where((block == BLOCKS * chan + i) & (holder == chan + step), 1.0, 0.0), axis=1, keepdims=True)
            for i in range(BLOCKS)
        ]
        return hits[0] * hits[1] * hits[2]

    most = jnp.max(jnp.maximum(all_three(first, 1.0), all_three(second, -1.0)))

    def total(hit, value=1.0):
        return jnp.sum(jnp.where(hit, value, 0.0))

    first = first - BLOCKS * me
    second = second - BLOCKS * me
    apart = holder - me
    mine = apart == 0.0

    def needs(hit, block):
        return [(total(hit & (block == float(i))) > 0.0).astype(jnp.int32) for i in range(BLOCKS)]

    to_right = needs(apart == 1.0, first)
    to_left = needs(apart == -1.0, second)
    of_left = needs(mine, first + BLOCKS)
    of_right = needs(mine, second - BLOCKS)
    earlier = lax.broadcasted_iota(jnp.int32, (128, 128), 0) < lax.broadcasted_iota(jnp.int32, (128, 128), 1)
    ranks = jnp.dot(
        jnp.broadcast_to(jnp.where(mine, 1.0, 0.0), (8, 128)).astype(jnp.bfloat16),
        jnp.where(earlier, 1.0, 0.0).astype(jnp.bfloat16),
        preferred_element_type=jnp.float32,
    )[0:1, :]
    number = total(mine).astype(jnp.int32)

    def spot(need, block, width):
        if width == BLOCKS:
            return block
        return jnp.where(block == 0, 0, jnp.where(block == 1, need[0], jnp.minimum(need[0] + need[1], width - 1)))

    def picks(need, width):
        if width == BLOCKS:
            return [jnp.int32(i) for i in range(BLOCKS)]
        n0, n1, n2 = [n > 0 for n in need]
        lowest = jnp.where(n0, 0, jnp.where(n1, 1, jnp.where(n2, 2, 0)))
        after = jnp.where(n0 & n1, 1, jnp.where(n2 & (n0 | n1), 2, lowest))
        return [lowest.astype(jnp.int32), after.astype(jnp.int32), jnp.int32(0)]

    flag[0] = most.astype(jnp.int32)
    for info, width in ((narrow, 2), (wide, BLOCKS)):
        for i, (right, left) in enumerate(zip(picks(to_right, width), picks(to_left, width))):
            info[LANES + i] = jnp.where(odd == 1, right, left)
            info[LANES + 3 + i] = jnp.where(odd == 1, left, right)
    for slot in range(PCAP):
        hit = mine & (ranks == float(slot))
        a = total(hit, first).astype(jnp.int32)
        b = total(hit, second).astype(jnp.int32)
        used = (number > slot).astype(jnp.int32)
        for info, width in ((narrow, 2), (wide, BLOCKS)):
            from_left = BLOCKS + odd * width
            from_right = BLOCKS + (1 - odd) * width
            info[FIRST + slot] = jnp.where(a < 0, from_left + spot(of_left, a + BLOCKS, width), a)
            info[SECOND + slot] = jnp.where(b >= BLOCKS, from_right + spot(of_right, b - BLOCKS, width), b)
            info[USED + slot] = used


def whitened(rows, basis):
    spectrum = jnp.dot(rows, basis, preferred_element_type=jnp.float32)
    power_mean = jnp.mean(spectrum * spectrum, axis=-1, keepdims=True)
    return (spectrum * lax.rsqrt(power_mean + 1e-06)).astype(jnp.bfloat16)


COST = pl.CostEstimate(flops=2 * 3 * ROWS * LENGTH * LENGTH, bytes_accessed=8 << 20, transcendentals=0)


def lane_copy(buf, block, lanes, way, spot, lsem):
    return pltpu.make_async_copy(buf.at[block], lanes[way].at[spot], lsem.at[way, spot])


def start_lanes(width, info, buf, block, lanes, lsem):
    for way in range(2):
        for spot in range(width):

            @pl.when(info[LANES + way * 3 + spot] == block)
            def _(way=way, spot=spot):
                lane_copy(buf, block, lanes, way, spot, lsem).start()


def wait_lanes(width, buf, lanes, lsem):
    for way in range(2):
        for spot in range(width):
            lane_copy(buf, 0, lanes, way, spot, lsem).wait()


def raw_lanes_kernel(width, info, x, one, two, buf, plain, xsem, lsem):
    loads = [pltpu.make_async_copy(x.at[block, :, 0], buf.at[block], xsem.at[block]) for block in range(BLOCKS)]
    for copy in loads:
        copy.start()
    for block, copy in enumerate(loads):
        copy.wait()
        plain[block] = buf[block].reshape(ROWS, LENGTH)
        start_lanes(width, info, plain, block, (one, two), lsem)
    wait_lanes(width, plain, (one, two), lsem)


def raw_lanes(width, info, x):
    lane = jax.ShapeDtypeStruct((width, ROWS, LENGTH), jnp.bfloat16)
    return pl.pallas_call(
        lambda *refs: raw_lanes_kernel(width, *refs),
        out_shape=(lane, lane),
        in_specs=[SMEM, HBM],
        out_specs=[ANY] * 2,
        scratch_shapes=[
            pltpu.VMEM((BLOCKS, 16, HALF, 2, LENGTH), jnp.bfloat16),
            pltpu.VMEM((BLOCKS, ROWS, LENGTH), jnp.bfloat16),
            pltpu.SemaphoreType.DMA((BLOCKS,)),
            pltpu.SemaphoreType.DMA((2, width)),
        ],
        compiler_params=PARAMS,
        cost_estimate=pl.CostEstimate(flops=0, bytes_accessed=4 << 20, transcendentals=0),
        name="raw_lanes",
    )(info, x)


def prepare_kernel(where, pairs, owner, x, narrow, wide, flag, deal, one, two, *scratch):
    pairs_here, owner_here, rows, psem, buf, laid, plain, xsem, dsem, lsem = scratch
    small = [
        pltpu.make_async_copy(pairs, pairs_here, psem.at[0]),
        pltpu.make_async_copy(owner, owner_here, psem.at[1]),
    ]
    for copy in small:
        copy.start()
    loads = [
        [pltpu.make_async_copy(x.at[block, :, chunk], buf.at[chunk, block], xsem.at[chunk, block]) for block in range(BLOCKS)]
        for chunk in range(CHUNKS)
    ]
    for copies in reversed(loads):
        for copy in copies:
            copy.start()
    deals = [
        [
            pltpu.make_async_copy(laid.at[block, z], deal.at[:, block, z], dsem.at[block, z])
            for z in range(2)
        ]
        for block in range(BLOCKS)
    ]
    for copy in small:
        copy.wait()
    fill_tables(where, pairs_here, owner_here, narrow, wide, flag, rows)
    for block in range(BLOCKS):
        loads[1][block].wait()
        laid[block] = buf[1, block].reshape(2, 8, 2 * HALF, LENGTH)
        for copy in deals[block]:
            copy.start()
    for block in range(BLOCKS):
        loads[0][block].wait()
        plain[block] = buf[0, block].reshape(ROWS, LENGTH)
        start_lanes(2, narrow, plain, block, (one, two), lsem)
    for copies in deals:
        for copy in copies:
            copy.wait()
    wait_lanes(2, plain, (one, two), lsem)


def prepare(where, pairs, owner, x):
    table = jax.ShapeDtypeStruct((TABLE,), jnp.int32)
    lane = jax.ShapeDtypeStruct((2, ROWS, LENGTH), jnp.bfloat16)
    return pl.pallas_call(
        prepare_kernel,
        out_shape=(
            table,
            table,
            jax.ShapeDtypeStruct((1,), jnp.int32),
            jax.ShapeDtypeStruct((8, BLOCKS, 2, 2 * HALF, LENGTH), jnp.bfloat16),
            lane,
            lane,
        ),
        in_specs=[SMEM, HBM, HBM, HBM],
        out_specs=[SMEM] * 3 + [ANY] * 3,
        scratch_shapes=[
            pltpu.VMEM((2, pairs.shape[0]), jnp.int32),
            pltpu.VMEM((1, pairs.shape[0]), jnp.int32),
            pltpu.VMEM((8, 128), jnp.float32),
            pltpu.SemaphoreType.DMA((2,)),
            pltpu.VMEM((CHUNKS, BLOCKS, 16, HALF, 2, LENGTH), jnp.bfloat16),
            pltpu.VMEM((BLOCKS, 2, 8, 2 * HALF, LENGTH), jnp.bfloat16),
            pltpu.VMEM((BLOCKS, ROWS, LENGTH), jnp.bfloat16),
            pltpu.SemaphoreType.DMA((CHUNKS, BLOCKS)),
            pltpu.SemaphoreType.DMA((BLOCKS, 2)),
            pltpu.SemaphoreType.DMA((2, 2)),
        ],
        compiler_params=ALL_VMEM,
        cost_estimate=pl.CostEstimate(flops=0, bytes_accessed=7 << 20, transcendentals=0),
        name="prepare",
    )(where, pairs.T, owner[None], x)


def taken(info, spot):
    hits = [
        (info[USED + slot] > 0) & ((info[FIRST + slot] == spot) | (info[SECOND + slot] == spot)) for slot in range(PCAP)
    ]
    return hits[0] | hits[1] | hits[2] | hits[3]


def spectra_kernel(count, base, at, info, x, basis, own, xbuf, spec, xsem, osem):
    def load(block):
        return pltpu.make_async_copy(x.at[at(block)], xbuf.at[block], xsem.at[block])

    def store(block):
        return pltpu.make_async_copy(spec.at[block], own.at[block], osem.at[block])

    for block in range(count):
        load(block).start()
    for block in range(count):
        load(block).wait()

        @pl.when(taken(info, base + block))
        def _(block=block):
            spec[block] = whitened(xbuf[block].reshape(ROWS, LENGTH), basis[...])

        store(block).start()
    for block in range(count):
        store(block).wait()


def spectra(count, base, at, shape, info, x, basis):
    return pl.pallas_call(
        lambda *refs: spectra_kernel(count, base, at, *refs),
        out_shape=jax.ShapeDtypeStruct((count, ROWS, LENGTH), jnp.bfloat16),
        in_specs=[SMEM, HBM, VMEM],
        out_specs=ANY,
        scratch_shapes=[
            pltpu.VMEM((count,) + shape, jnp.bfloat16),
            pltpu.VMEM((count, ROWS, LENGTH), jnp.bfloat16),
            pltpu.SemaphoreType.DMA((count,)),
            pltpu.SemaphoreType.DMA((count,)),
        ],
        compiler_params=PARAMS,
        cost_estimate=COST,
        name="spectra",
    )(info, x, basis)


def dealt_kernel(width, info, x, basis, one, two, spec, lsem):
    for block in range(BLOCKS):
        picks = [info[LANES + way * 3 + spot] == block for way in range(2) for spot in range(width)]
        wanted = picks[0]
        for pick in picks[1:]:
            wanted = wanted | pick

        @pl.when(wanted)
        def _(block=block):
            spec[block] = whitened(x[:, block].reshape(ROWS, LENGTH), basis[...])
            start_lanes(width, info, spec, block, (one, two), lsem)

    wait_lanes(width, spec, (one, two), lsem)


def dealt_lanes(width, info, x, basis):
    lane = jax.ShapeDtypeStruct((width, ROWS, LENGTH), jnp.bfloat16)
    return pl.pallas_call(
        lambda *refs: dealt_kernel(width, *refs),
        out_shape=(lane, lane),
        in_specs=[SMEM, VMEM, VMEM],
        out_specs=[HBM] * 2,
        scratch_shapes=[
            pltpu.VMEM((BLOCKS, ROWS, LENGTH), jnp.bfloat16),
            pltpu.SemaphoreType.DMA((2, width)),
        ],
        compiler_params=PARAMS,
        cost_estimate=COST,
        name="dealt_lanes",
    )(info, x, basis)


def dealt_own_kernel(x, basis, own):
    for block in range(BLOCKS):
        own[block] = whitened(x[:, block].reshape(ROWS, LENGTH), basis[...])


def dealt_spectra(x, basis):
    return pl.pallas_call(
        dealt_own_kernel,
        out_shape=jax.ShapeDtypeStruct((BLOCKS, ROWS, LENGTH), jnp.bfloat16),
        in_specs=[VMEM, VMEM],
        out_specs=VMEM,
        compiler_params=PARAMS,
        cost_estimate=COST,
        name="dealt_spectra",
    )(x, basis)


def parts(read, at, lane):
    a_re, a_im, b_re, b_im = [
        read(operand, at, pl.ds(start + lane * 128, 128)).astype(jnp.float32)
        for operand in range(2)
        for start in (0, BINS)
    ]
    return a_re * b_re + a_im * b_im, a_im * b_re - a_re * b_im


def pair_sums(acc):
    return acc[pl.ds(0, HALF, 2), :] + acc[pl.ds(1, HALF, 2), :]


def tile(index):
    return pl.ds(pl.multiple_of(index * 2 * HALF, 2 * HALF), 2 * HALF)


def raw_products_kernel(width, info, basis, own, one, two, out, xbuf, buf, acc, xsem, osem):
    loads = [pltpu.make_async_copy(two.at[spot], xbuf.at[spot], xsem.at[spot]) for spot in range(width)]
    ready = [
        pltpu.make_async_copy(own, buf.at[pl.ds(0, BLOCKS)], osem.at[0]),
        pltpu.make_async_copy(one, buf.at[pl.ds(BLOCKS, width)], osem.at[1]),
    ]
    for copy in loads + ready:
        copy.start()
    for spot, copy in enumerate(loads):
        copy.wait()

        @pl.when(taken(info, BLOCKS + width + spot))
        def _(spot=spot):
            buf[BLOCKS + width + spot] = whitened(xbuf[spot].reshape(ROWS, LENGTH), basis[...])

    for copy in ready:
        copy.wait()

    @pl.loop(0, PCAP)
    def _(slot):
        spots = info[FIRST + slot], info[SECOND + slot]

        def read(operand, at, part):
            return buf[spots[operand], at, part]

        @pl.when(info[USED + slot] > 0)
        def _():
            @pl.loop(0, 8)
            def _(peer):
                for lane in range(BINS // 128):
                    for z in range(2):
                        acc[lane, z, 0], acc[lane, z, 1] = parts(read, tile(z * 8 + (peer + 4) % 8), lane)
                    for part in range(2):
                        sums = [pair_sums(acc.at[lane, z, part]) for z in range(2)]
                        out[peer, slot, :, pl.ds(part * BINS + lane * 128, 128)] = jnp.concatenate(
                            sums, axis=0
                        ).astype(jnp.bfloat16)

        @pl.when(info[USED + slot] == 0)
        def _():
            @pl.loop(0, 8)
            def _(peer):
                out[peer, slot] = jnp.zeros((2 * HALF, LENGTH), jnp.bfloat16)


def raw_products(width, info, basis, own, one, two):
    return pl.pallas_call(
        lambda *refs: raw_products_kernel(width, *refs),
        out_shape=jax.ShapeDtypeStruct((8, PCAP, 2 * HALF, LENGTH), jnp.bfloat16),
        in_specs=[SMEM, VMEM, ANY, ANY, HBM],
        out_specs=VMEM,
        scratch_shapes=[
            pltpu.VMEM((width, ROWS, LENGTH), jnp.bfloat16),
            pltpu.VMEM((BLOCKS + 2 * width, ROWS, LENGTH), jnp.bfloat16),
            pltpu.VMEM((BINS // 128, 2, 2, 2 * HALF, 128), jnp.float32),
            pltpu.SemaphoreType.DMA((width,)),
            pltpu.SemaphoreType.DMA((2,)),
        ],
        compiler_params=PARAMS,
        cost_estimate=COST,
        name="raw_products",
    )(info, basis, own, one, two)


def dealt_products_kernel(width, info, own, one, two, out, buf, acc, sems):
    def start(slot, operand, spot):
        to, sem = buf.at[slot, operand], sems.at[slot, operand]

        @pl.when(spot < BLOCKS)
        def _():
            pltpu.make_async_copy(own.at[spot], to, sem).start()

        @pl.when((spot >= BLOCKS) & (spot < BLOCKS + width))
        def _():
            pltpu.make_async_copy(one.at[spot - BLOCKS], to, sem).start()

        @pl.when(spot >= BLOCKS + width)
        def _():
            pltpu.make_async_copy(two.at[spot - BLOCKS - width], to, sem).start()

    for slot in range(PCAP):

        @pl.when(info[USED + slot] > 0)
        def _(slot=slot):
            start(slot, 0, info[FIRST + slot])
            start(slot, 1, info[SECOND + slot])

    @pl.loop(0, PCAP)
    def _(slot):
        def read(operand, at, part):
            return buf[slot, operand, at, part]

        @pl.when(info[USED + slot] > 0)
        def _():
            for operand in range(2):
                pltpu.make_async_copy(own.at[0], buf.at[slot, operand], sems.at[slot, operand]).wait()

            @pl.loop(0, 2)
            def _(z):
                for lane in range(BINS // 128):
                    real, imag = parts(read, tile(z), lane)
                    for source in range(1, 8):
                        re, im = parts(read, tile(source * 2 + z), lane)
                        real, imag = real + re, imag + im
                    acc[lane, 0], acc[lane, 1] = real, imag
                    for part in range(2):
                        out[z, slot, :, pl.ds(part * BINS + lane * 128, 128)] = pair_sums(acc.at[lane, part])

        @pl.when(info[USED + slot] == 0)
        def _():
            for z in range(2):
                out[z, slot] = jnp.zeros((HALF, LENGTH), jnp.float32)


def dealt_products(width, info, own, one, two):
    return pl.pallas_call(
        lambda *refs: dealt_products_kernel(width, *refs),
        out_shape=jax.ShapeDtypeStruct((2, PCAP, HALF, LENGTH), jnp.float32),
        in_specs=[SMEM] + [ANY] * 3,
        out_specs=VMEM,
        scratch_shapes=[
            pltpu.VMEM((PCAP, 2, ROWS, LENGTH), jnp.bfloat16),
            pltpu.VMEM((BINS // 128, 2, 2 * HALF, 128), jnp.float32),
            pltpu.SemaphoreType.DMA((PCAP, 2)),
        ],
        compiler_params=PARAMS,
        cost_estimate=pl.CostEstimate(flops=1 << 25, bytes_accessed=8 << 20, transcendentals=0),
        name="dealt_products",
    )(info, own, one, two)


def path(records, info, deal, raw, width):
    far = lax.axis_index("win") // 8
    basis = jnp.asarray(basis_table())
    x = records.reshape(BLOCKS, 16, CHUNKS, HALF, 2, LENGTH)
    chip_groups = [[z * 8 + j for j in range(8)] for z in range(2)]
    turned_groups = [[z * 8 + (j + 4) % 8 for j in range(8)] for z in range(2)]
    far_groups = [[z * 8 + j for z in range(2)] for j in range(8)]

    dealt = lax.all_to_all(deal, "win", 0, 0, tiled=True, axis_index_groups=chip_groups)
    if raw is None:
        raw = raw_lanes(width, info, x)
    raw_one, raw_two = [lax.ppermute(lane, "chan", swap) for lane, swap in zip(raw, SWAPS)]
    sent = dealt_lanes(width, info, dealt, basis)
    raw_basis, *sent = lax.optimization_barrier((basis, *sent))
    came = [lax.ppermute(lane, "chan", swap) for lane, swap in zip(sent, SWAPS)]
    own = spectra(BLOCKS, 0, lambda block: (block, slice(None), 0), (16, HALF, 2, LENGTH), info, x, basis)
    one = spectra(width, BLOCKS, lambda spot: (spot,), (ROWS, LENGTH), info, raw_one, raw_basis)

    part = raw_products(width, info, raw_basis, own, one, raw_two)
    first = lax.all_to_all(part, "win", 0, 0, tiled=True, axis_index_groups=turned_groups)
    dealt, part = lax.optimization_barrier((dealt, part))
    second = dealt_products(width, info, dealt_spectra(dealt, basis), *came)
    first, second = lax.optimization_barrier((first, second))
    first = jnp.sum(first.astype(jnp.float32), axis=0).reshape(PCAP, 2, HALF, LENGTH)

    def half(at):
        return jnp.concatenate(
            [
                lax.dynamic_index_in_dim(first, at, axis=1, keepdims=False),
                lax.dynamic_index_in_dim(second, at, axis=0, keepdims=False),
            ],
            axis=1,
        )

    give = half(1 - far).astype(jnp.bfloat16)

    def swapped(slots):
        got = lax.all_gather(give[:slots], "win", axis=0, tiled=True, axis_index_groups=far_groups)
        got = lax.dynamic_slice_in_dim(got, (1 - far) * slots, slots, axis=0).astype(jnp.float32)
        return jnp.concatenate([got, jnp.zeros((PCAP - slots,) + got.shape[1:], jnp.float32)], axis=0)

    got = lax.cond(info[USED + 2] > 0, lambda: swapped(PCAP), lambda: swapped(PCAP // 2))
    return half(far) + got


def local(records, pairs, owner):
    where = lax.axis_index("chan")[None].astype(jnp.int32)
    x = records.reshape(BLOCKS, 16, CHUNKS, HALF, 2, LENGTH)
    narrow, wide, three, deal, *raw = prepare(where, pairs, owner, x)
    return lax.cond(
        three.reshape(()) == 0,
        lambda: path(records, narrow, deal, raw, 2),
        lambda: path(records, wide, deal, None, BLOCKS),
    )


def solution(mesh):
    return jax.shard_map(
        local,
        mesh=mesh,
        in_specs=(P("chan", None, "win", None), P(), P()),
        out_specs=P("chan", "win", None),
        check_vma=False,
    )
```
